512 devices in a mesh: dp: 16 (over y, x), tensor: 32 (over z, core).
Axes of the slice: x: 4, y: 4, z: 16, core: 2. Of those that a mesh axis runs over, the one named last changes fastest.
Arguments:
- activations: bfloat16 [2048, 8192], P('dp'), may hold values from -6 to 6
- cotangent: bfloat16 [2, 2048, 28672], P(None, 'dp', 'tensor'), may hold values from -6 to 6
- weights: bfloat16 [2, 8192, 28672], P(None, 'dp', 'tensor'), may hold values from -0.0625 to 0.0625
- proj_basis: bfloat16 [8192, 512], replicated, may hold values from -0.0625 to 0.0625
- first_moment: float32 [2, 512, 28672], P(None, 'dp', 'tensor'), may hold values from -6 to 6
- second_moment: float32 [2, 512, 28672], P(None, 'dp', 'tensor'), may hold values from 1 to 20
- step_number: int32 [1], replicated, may hold values from 1 to 999
Outputs:
- input_grad: bfloat16 [2048, 8192], P(None, 'dp')
- update: bfloat16 [2, 8192, 28672], P(None, 'dp', 'tensor')
- first_new: float32 [2, 512, 28672], P(None, 'dp', 'tensor')
- second_new: float32 [2, 512, 28672], P(None, 'dp', 'tensor')
The draws below stay inside these ranges and needn't reach their ends.
All inputs are finite; a program needn't handle non-finite values.
Results may differ from the reference program's by a relative error of at most 0.0051.
Values may be sent and summed in bfloat16 or wider, within the bound.
A program may use at most 128 MiB of HBM per device.

```python
import math
import jax
import jax.numpy as jnp
from jax import lax

D = 8192
FF = 28672
RANK = 512
TOKENS = 2048


def shard_levels(stream_key, shape, shards, least, high):
    factor_of, own = 1.0, jax.random.fold_in(stream_key, 6)
    for position, blocks in shards:
        steps = jnp.exp(jax.random.uniform(jax.random.fold_in(own, position), (blocks,), jnp.float32, least / len(shards), high / len(shards)))
        factor_of = factor_of * jnp.repeat(steps, shape[position] // blocks).reshape([-1 if axis == position else 1 for axis in range(len(shape))])
    return factor_of


def gaussian(own_key, extent, scale, reach, pieces=(), kind=jnp.bfloat16):
    drawn = jax.random.normal(own_key, extent, jnp.float32) * scale
    if len(pieces) > 0:
        drawn = shard_levels(own_key, extent, pieces, -0.22, 0.18) * drawn
    return jnp.clip(drawn, min=-reach, max=reach).astype(kind)


def setup_inputs(seed: int = 0) -> dict:
    keys = jax.random.split(jax.random.key(seed), 8)
    return {
        "activations": gaussian(keys[0], (TOKENS, D), 1.0, 6.0, ((0, 16),)),
        "cotangent": gaussian(keys[1], (2, TOKENS, FF), 1.0, 6.0, ((1, 16), (2, 32))),
        "weights": gaussian(keys[2], (2, D, FF), D ** -0.5, 0.0625, ((1, 16), (2, 32))),
        "proj_basis": gaussian(keys[3], (D, RANK), D ** -0.5, 0.0625),
        "first_moment": gaussian(keys[4], (2, RANK, FF), 1.0, 6.0, ((1, 16), (2, 32)), jnp.float32),
        "second_moment": jnp.clip(jnp.exp(math.log(20.0) - 2.9957323 * jax.random.uniform(keys[5], (2, RANK, FF), jnp.float32) ** shard_levels(keys[5], (2, RANK, FF), ((1, 16), (2, 32)), -0.2, 0.2)), 1.0, 20.0),
        "step_number": jax.random.randint(keys[6], (1,), 1, 1000).astype(jnp.int32),
    }


beta_one = 0.9
beta_two = 0.999
adam_eps = 1e-08

def reference(activations, cotangent, weights, proj_basis, first_moment, second_moment, step_number):
    gate_part = jnp.dot(cotangent[0], weights[0].T, preferred_element_type=jnp.float32)
    up_part = jnp.dot(cotangent[1], weights[1].T, preferred_element_type=jnp.float32)
    input_grad = (gate_part + up_part).astype(jnp.bfloat16)
    coords = jnp.dot(activations, proj_basis, preferred_element_type=jnp.float32).astype(jnp.bfloat16)
    projected = jnp.stack([jnp.dot(coords.T, cotangent[0], preferred_element_type=jnp.float32), jnp.dot(coords.T, cotangent[1], preferred_element_type=jnp.float32)])
    step_value = step_number[0].astype(jnp.float32)
    first_new = beta_one * first_moment + (1.0 - beta_one) * projected
    second_new = beta_two * second_moment + (1.0 - beta_two) * projected * projected
    first_fix = 1.0 - jnp.power(jnp.float32(beta_one), step_value)
    second_fix = 1.0 - jnp.power(jnp.float32(beta_two), step_value)
    normalized = first_new / first_fix / (jnp.sqrt(second_new / second_fix) + adam_eps)
    basis_wide = proj_basis.astype(jnp.float32)
    update = jnp.stack([jnp.dot(basis_wide, normalized[0], precision=lax.Precision.HIGHEST).astype(jnp.bfloat16), jnp.dot(basis_wide, normalized[1], precision=lax.Precision.HIGHEST).astype(jnp.bfloat16)])
    return (input_grad, update, first_new, second_new)
```

```python
import functools
import math

import jax
import jax.numpy as jnp
from jax import lax
from jax.experimental import pallas as pl
from jax.experimental.pallas import tpu as pltpu
from jax.sharding import PartitionSpec as P

MESH = pl.DeviceIdType.MESH
beta_one = 0.9
beta_two = 0.999
adam_eps = 1e-08

F32 = jnp.float32
BF16 = jnp.bfloat16

ROUNDS = (
    ((0, 0), (0, 1), (0, 3), (0, 2)),
    ((1, 0), (3, 0), (2, 0), (1, 1)),
    ((1, 3), (3, 1), (3, 3), (1, 2)),
    ((3, 2), (2, 1), (2, 3), (2, 2)),
)


def remote(src, dst, send, recv, dev):
    return pltpu.make_async_remote_copy(
        src_ref=src, dst_ref=dst, send_sem=send, recv_sem=recv, device_id=dev, device_id_type=MESH
    )


class Gather:
    def __init__(self, buf, full, half, send_full, send_half, x, y):
        self.buf, self.full, self.half = buf, full, half
        self.send_full, self.send_half = send_full, send_half
        self.x, self.y = x, y
        self.rows = buf.shape[2] // 2
        self.sent = []

    def piece(self, g, u, v):
        dy, dx = (v, u) if g == 0 else (u, v)
        return lax.rem(self.y + dy, 4) * 4 + lax.rem(self.x + dx, 4)

    def device(self, g, axis, delta):
        along_x = (axis == 1) == (g == 0)
        if along_x:
            return {"dp": self.y * 4 + lax.rem(self.x + delta, 4)}
        return {"dp": lax.rem(self.y + delta, 4) * 4 + self.x}

    def send(self, g, axis, u, v, delta):
        p = self.piece(g, u, v)
        slot = 0 if axis == 1 else 1 + u
        ref = self.buf.at[g, p]
        copy = remote(
            ref, ref, self.send_full.at[g, slot, delta // 2], self.full.at[g, p],
            self.device(g, axis, delta),
        )
        copy.start()
        self.sent.append(copy)

    def relay(self, g, axis, u, v):
        off = u if axis == 1 else v
        delta, h = (3, 1) if off == 1 else (1, 0)
        p = self.piece(g, u, v)
        slot = 0 if axis == 1 else 1 + u
        ref = self.buf.at[g, p, pl.ds(h * self.rows, self.rows)]
        copy = remote(
            ref, ref, self.send_half.at[g, slot, h], self.half.at[g, p, h],
            self.device(g, axis, delta),
        )
        copy.start()
        self.sent.append(copy)

    def wait_full(self, g, u, v):
        p = self.piece(g, u, v)
        ref = self.buf.at[g, p]
        remote(
            ref, ref, self.send_full.at[g, 0, 0], self.full.at[g, p], self.device(g, 1, 1)
        ).wait_recv()

    def wait_halves(self, g, u, v):
        p = self.piece(g, u, v)
        for h in (0, 1):
            ref = self.buf.at[g, p, pl.ds(h * self.rows, self.rows)]
            remote(
                ref, ref, self.send_half.at[g, 0, 0], self.half.at[g, p, h], self.device(g, 1, 1)
            ).wait_recv()

    def start(self):
        for axis in (1, 2):
            for g in (0, 1):
                for delta in (1, 3):
                    self.send(g, axis, 0, 0, delta)

    def near(self):
        for u in (1, 3):
            for g in (0, 1):
                self.wait_full(g, u, 0)
                self.relay(g, 1, u, 0)
            for g in (0, 1):
                self.wait_full(g, 0, u)
                self.relay(g, 2, 0, u)
            for g in (0, 1):
                for delta in (1, 3):
                    self.send(g, 2, u, 0, delta)

    def far(self):
        for g in (0, 1):
            self.wait_halves(g, 2, 0)
            for delta in (1, 3):
                self.send(g, 2, 2, 0, delta)
        for g in (0, 1):
            self.wait_halves(g, 0, 2)

    def cross(self, u):
        for v in (1, 3):
            for g in (0, 1):
                self.wait_full(g, u, v)
                self.relay(g, 2, u, v)

    def rest(self, u):
        for g in (0, 1):
            self.wait_halves(g, u, 2)

    def drain(self):
        for copy in self.sent:
            copy.wait_send()


def pick(index, values):
    out = values[0]
    for i in range(1, len(values)):
        out = jnp.where(index == i, values[i], out)
    return out


def kernel(
    act_h, cot_h, w_h, basis_h, m1_h, m2_h, step_s,
    ig_h, upd_h, fn_h, sn_h,
    act, basis, w, m1, m2, cot, ct_own, ct, norm, acc, tmp, kept, sib_s, sib_r,
    a_s, a_r, b_s, b_r, out, ig, upd,
    load_sem, ct_send, ct_recv, c_full, c_half, c_sf, c_sh, n_full, n_half, n_sf, n_sh,
    sib_ss, sib_rs, za_s, za_r, zb_s, zb_r, zc_s, zc_r, zd_s, zd_r, ze_s, ze_r, store_sem,
):
    dp = lax.axis_index("dp")
    tensor = lax.axis_index("tensor")
    y, x = lax.div(dp, 4), lax.rem(dp, 4)
    z, c = lax.div(tensor, 2), lax.rem(tensor, 2)
    oc = 1 - c
    r0, q0 = lax.rem(z, 4), lax.div(z, 4)

    def along_z(delta):
        return {"tensor": lax.rem(z + delta + 16, 16) * 2 + c}

    sibling = {"tensor": z * 2 + oc}

    loads = [
        pltpu.make_async_copy(cot_h.at[0], cot.at[0, dp], load_sem.at[0]),
        pltpu.make_async_copy(cot_h.at[1], cot.at[1, dp], load_sem.at[1]),
        pltpu.make_async_copy(act_h, act, load_sem.at[2]),
        pltpu.make_async_copy(basis_h, basis, load_sem.at[3]),
        pltpu.make_async_copy(w_h, w, load_sem.at[4]),
        pltpu.make_async_copy(m1_h, m1, load_sem.at[5]),
        pltpu.make_async_copy(m2_h, m2, load_sem.at[6]),
    ]
    for load in loads:
        load.start()

    barrier = pltpu.get_barrier_semaphore()

    def greet(d, carry):
        pl.semaphore_signal(
            barrier, inc=1, device_id={"dp": lax.rem(dp + d, 16)}, device_id_type=MESH
        )
        return carry

    lax.fori_loop(1, 16, greet, 0)
    for delta in (1, -1, 2, -2, 4, -4, 8):
        pl.semaphore_signal(barrier, inc=1, device_id=along_z(delta), device_id_type=MESH)
    pl.semaphore_signal(barrier, inc=1, device_id=sibling, device_id_type=MESH)
    pl.semaphore_wait(barrier, 23)

    gather = Gather(cot, c_full, c_half, c_sf, c_sh, x, y)
    loads[0].wait()
    loads[1].wait()
    gather.start()

    loads[2].wait()
    loads[3].wait()

    def coord_step(i, total):
        cols = pl.ds(pl.multiple_of(i * 1024, 1024), 1024)
        return total + jnp.dot(act[:, cols], basis[cols, :], preferred_element_type=F32)

    coords = lax.fori_loop(0, 8, coord_step, jnp.zeros((128, 512), F32))
    ct_own[...] = coords.T.astype(BF16)

    def ct_copy(d):
        to = lax.rem(dp + d, 16)
        rows = pl.ds(pl.multiple_of(to * 32, 32), 32)
        return remote(ct_own.at[rows], ct.at[dp], ct_send.at[d], ct_recv.at[dp], {"dp": to})

    def ct_start(d, carry):
        ct_copy(d).start()
        return carry

    lax.fori_loop(1, 16, ct_start, 0)
    ct[dp] = ct_own[pl.ds(pl.multiple_of(dp * 32, 32), 32), :]

    gather.near()

    def ct_wait(d, carry):
        s = lax.rem(dp + d, 16)
        remote(ct.at[s], ct.at[s], ct_send.at[d], ct_recv.at[s], {"dp": s}).wait_recv()
        return carry

    lax.fori_loop(1, 16, ct_wait, 0)
    acc[...] = jnp.zeros_like(acc)
    loads[4].wait()

    def places(k):
        return [lax.rem(y + dy, 4) * 4 + lax.rem(x + dx, 4) for dy, dx in ROUNDS[k]]

    shifts = (1, 15, pick(c, [2, 14]))
    sends = []

    def project(k):
        spots = places(k)

        def step(q, carry):
            p = pick(q, spots)
            for g in (0, 1):
                acc[g] += jnp.dot(ct[p], cot[g, p], preferred_element_type=F32)
            return carry

        lax.fori_loop(0, 4, step, 0)

    def z1(k):
        spots = places(k)

        def step(q, carry):
            p = pick(q, spots)
            part = lax.dot_general(
                cot[0, p], w[0], (((1,), (1,)), ((), ())), preferred_element_type=F32
            )
            part += lax.dot_general(
                cot[1, p], w[1], (((1,), (1,)), ((), ())), preferred_element_type=F32
            )
            tmp[0] = part[:64]
            tmp[1] = part[64:]
            for r in range(4):
                kept[k, r, q] = tmp[c, :, r * 128 : (r + 1) * 128]
                sib_s[k, r, q] = tmp[oc, :, r * 128 : (r + 1) * 128].astype(BF16)
            return carry

        lax.fori_loop(0, 4, step, 0)
        copy = remote(sib_s.at[k], sib_r.at[k], sib_ss.at[k], sib_rs.at[k], sibling)
        copy.start()
        sends.append(copy)

    def z2(k):
        remote(sib_s.at[k], sib_r.at[k], sib_ss.at[k], sib_rs.at[k], sibling).wait_recv()

        def step(r, carry):
            total = kept[k, r] + sib_r[k, r].astype(F32)
            kept[k, r] = total
            a_s[k, r] = total.astype(BF16)
            return carry

        lax.fori_loop(0, 4, step, 0)
        for i, delta in enumerate(shifts):
            copy = remote(
                a_s.at[k, lax.rem(z + delta, 4)], a_r.at[k, i], za_s.at[k, i], za_r.at[k, i],
                along_z(delta),
            )
            copy.start()
            sends.append(copy)

    def z3(k):
        total = kept[k, r0]
        for i in range(3):
            remote(a_r.at[k, i], a_r.at[k, i], za_s.at[k, i], za_r.at[k, i], sibling).wait_recv()
            total = total + a_r[k, i].astype(F32)
        kept[k, r0] = total
        b_s[k] = total.astype(BF16)
        for i, steps in enumerate((1, 3, 2)):
            copy = remote(
                b_s.at[k, lax.rem(q0 + steps, 4)], b_r.at[k, i], zb_s.at[k, i], zb_r.at[k, i],
                along_z(4 * steps),
            )
            copy.start()
            sends.append(copy)

    def z4(k):
        total = kept[k, r0, q0]
        for i in range(3):
            remote(b_r.at[k, i], b_r.at[k, i], zb_s.at[k, i], zb_r.at[k, i], sibling).wait_recv()
            total = total + b_r[k, i].astype(F32)
        out[k, c, r0, q0] = total.astype(BF16)
        ref = out.at[k, c, r0, q0]
        for i, steps in enumerate((1, 3, 2)):
            copy = remote(ref, ref, zc_s.at[k, i], zc_r.at[k, i], along_z(4 * steps))
            copy.start()
            sends.append(copy)

    def z5(k):
        for i, steps in enumerate((1, 3, 2)):
            ref = out.at[k, c, r0, lax.rem(q0 + 4 - steps, 4)]
            remote(ref, ref, zc_s.at[k, i], zc_r.at[k, i], sibling).wait_recv()
        ref = out.at[k, c, r0]
        for i, delta in enumerate(shifts):
            copy = remote(ref, ref, zd_s.at[k, i], zd_r.at[k, i], along_z(delta))
            copy.start()
            sends.append(copy)

    def z6(k):
        for i, delta in enumerate(shifts):
            ref = out.at[k, c, lax.rem(z + 16 - delta, 4)]
            remote(ref, ref, zd_s.at[k, i], zd_r.at[k, i], sibling).wait_recv()
        ref = out.at[k, c]
        copy = remote(ref, ref, ze_s.at[k], ze_r.at[k], sibling)
        copy.start()
        sends.append(copy)

    def z7(k):
        ref = out.at[k, oc]
        remote(ref, ref, ze_s.at[k], ze_r.at[k], sibling).wait_recv()
        spots = places(k)

        def step(q, carry):
            p = pick(q, spots)
            for half in range(2):
                rows = pl.ds(pl.multiple_of(p * 128 + half * 64, 64), 64)
                for r in range(4):
                    ig[rows, r * 128 : (r + 1) * 128] = out[k, half, r, q]
            rows = pl.ds(pl.multiple_of(p * 128, 128), 128)
            pltpu.make_async_copy(ig.at[rows], ig_h.at[rows], store_sem.at[k, q]).start()
            return carry

        lax.fori_loop(0, 4, step, 0)

    def stored(k):
        spots = places(k)

        def step(q, carry):
            rows = pl.ds(pl.multiple_of(pick(q, spots) * 128, 128), 128)
            pltpu.make_async_copy(ig.at[rows], ig_h.at[rows], store_sem.at[k, q]).wait()
            return carry

        lax.fori_loop(0, 4, step, 0)

    gather.far()
    z1(0)
    z2(0)
    project(0)
    gather.cross(1)
    z1(1)
    z3(0)
    z2(1)
    project(1)
    gather.cross(3)
    z4(0)
    z3(1)
    gather.cross(2)
    gather.rest(1)
    z1(2)
    z2(2)
    project(2)
    z5(0)
    z4(1)
    gather.rest(3)
    gather.rest(2)
    project(3)

    loads[5].wait()
    loads[6].wait()
    step_value = jnp.full((1, 1), step_s[0].astype(F32), F32)
    first_fix = 1.0 - jnp.exp(step_value * math.log(beta_one))
    second_fix = 1.0 - jnp.exp(step_value * math.log(beta_two))
    for g in (0, 1):
        projected = acc[g]
        first = beta_one * m1[g] + (1.0 - beta_one) * projected
        second = beta_two * m2[g] + (1.0 - beta_two) * projected * projected
        m1[g] = first
        m2[g] = second
        norm[g, dp] = (first / first_fix / (jnp.sqrt(second / second_fix) + adam_eps)).astype(BF16)
    ngather = Gather(norm, n_full, n_half, n_sf, n_sh, x, y)
    ngather.start()
    stores = [
        pltpu.make_async_copy(m1, fn_h, load_sem.at[5]),
        pltpu.make_async_copy(m2, sn_h, load_sem.at[6]),
    ]
    for store in stores:
        store.start()

    z1(3)
    z2(3)
    z3(2)
    z6(0)
    z5(1)
    ngather.near()
    z3(3)
    z4(2)
    ngather.far()
    z7(0)
    z6(1)
    z4(3)
    z5(2)
    ngather.cross(1)
    ngather.cross(3)
    ngather.cross(2)
    z5(3)
    z7(1)
    z6(2)
    for u in (1, 3, 2):
        ngather.rest(u)

    rows = pl.ds(pl.multiple_of(dp * 512, 512), 512)
    for g in (0, 1):
        upd[g] = jnp.dot(
            basis[rows, :], norm[g].reshape(512, 896), preferred_element_type=F32
        ).astype(BF16)
        store = pltpu.make_async_copy(upd.at[g], upd_h.at[g], load_sem.at[g])
        store.start()
        stores.append(store)
    z6(3)
    z7(2)
    z7(3)

    gather.drain()
    ngather.drain()
    for copy in sends:
        copy.wait_send()

    def ct_drain(d, carry):
        ct_copy(d).wait_send()
        return carry

    lax.fori_loop(1, 16, ct_drain, 0)
    for store in stores:
        store.wait()
    for k in range(4):
        stored(k)


def local(activations, cotangent, weights, proj_basis, first_moment, second_moment, step_number):
    any_spec = pl.BlockSpec(memory_space=pl.ANY)
    dma = pltpu.SemaphoreType.DMA
    return pl.pallas_call(
        kernel,
        out_shape=(
            jax.ShapeDtypeStruct((2048, 512), BF16),
            jax.ShapeDtypeStruct((2, 512, 896), BF16),
            jax.ShapeDtypeStruct((2, 32, 896), F32),
            jax.ShapeDtypeStruct((2, 32, 896), F32),
        ),
        in_specs=[any_spec] * 6 + [pl.BlockSpec(memory_space=pltpu.SMEM)],
        out_specs=[any_spec] * 4,
        scratch_shapes=[
            pltpu.VMEM((128, 8192), BF16),
            pltpu.VMEM((8192, 512), BF16),
            pltpu.VMEM((2, 512, 896), BF16),
            pltpu.VMEM((2, 32, 896), F32),
            pltpu.VMEM((2, 32, 896), F32),
            pltpu.VMEM((2, 16, 128, 896), BF16),
            pltpu.VMEM((512, 128), BF16),
            pltpu.VMEM((16, 32, 128), BF16),
            pltpu.VMEM((2, 16, 32, 896), BF16),
            pltpu.VMEM((2, 32, 896), F32),
            pltpu.VMEM((2, 64, 512), F32),
            pltpu.VMEM((4, 4, 4, 64, 128), F32),
            pltpu.VMEM((4, 4, 4, 64, 128), BF16),
            pltpu.VMEM((4, 4, 4, 64, 128), BF16),
            pltpu.VMEM((4, 4, 4, 64, 128), BF16),
            pltpu.VMEM((4, 3, 4, 64, 128), BF16),
            pltpu.VMEM((4, 4, 64, 128), BF16),
            pltpu.VMEM((4, 3, 64, 128), BF16),
            pltpu.VMEM((4, 2, 4, 4, 64, 128), BF16),
            pltpu.VMEM((2048, 512), BF16),
            pltpu.VMEM((2, 512, 896), BF16),
            dma((7,)),
            dma((16,)), dma((16,)),
            dma((2, 16)), dma((2, 16, 2)), dma((2, 5, 2)), dma((2, 5, 2)),
            dma((2, 16)), dma((2, 16, 2)), dma((2, 5, 2)), dma((2, 5, 2)),
            dma((4,)), dma((4,)),
            dma((4, 3)), dma((4, 3)),
            dma((4, 3)), dma((4, 3)),
            dma((4, 3)), dma((4, 3)),
            dma((4, 3)), dma((4, 3)),
            dma((4,)), dma((4,)),
            dma((4, 4)),
        ],
        compiler_params=pltpu.CompilerParams(
            collective_id=0, has_side_effects=True, vmem_limit_bytes=60 << 20
        ),
        cost_estimate=pl.CostEstimate(
            flops=6_100_000_000, bytes_accessed=24_000_000, transcendentals=60_000
        ),
    )(activations, cotangent, weights, proj_basis, first_moment, second_moment, step_number)


def solution(mesh):
    return jax.shard_map(
        local,
        mesh=mesh,
        in_specs=(
            P("dp", None),
            P(None, "dp", "tensor"),
            P(None, "dp", "tensor"),
            P(),
            P(None, "dp", "tensor"),
            P(None, "dp", "tensor"),
            P(),
        ),
        out_specs=(
            P(None, "dp"),
            P(None, "dp", "tensor"),
            P(None, "dp", "tensor"),
            P(None, "dp", "tensor"),
        ),
        check_vma=False,
    )
```

```python
import functools
import math

import jax
import jax.numpy as jnp
from jax import lax
from jax.experimental import pallas as pl
from jax.experimental.pallas import tpu as pltpu
from jax.sharding import PartitionSpec as P

MESH = pl.DeviceIdType.MESH
beta_one = 0.9
beta_two = 0.999
adam_eps = 1e-08

F32 = jnp.float32
BF16 = jnp.bfloat16

ROUNDS = (
    ((0, 0), (0, 1), (0, 3), (1, 0)),
    ((3, 0), (0, 2), (2, 0), (3, 3), (3, 1)),
    ((1, 3), (1, 1)),
    ((3, 2), (1, 2), (2, 3)),
    ((2, 1), (2, 2)),
)
RELAYED = (True, True, True, False, False)
ORDER = (
    "cstart", "coords", "ct", "c030", "c010", "c130", "c110", "c103", "c101", "c003", "c001",
    "z1_0", "c020", "ctw", "pj_0", "c033", "c031", "z2_0", "c133", "c131", "z2b_0", "c013", "c011",
    "c113", "c111", "c120", "z1_2", "z3_0", "c102", "pj_2", "c002", "z1_1", "c132", "z3b_0", "z2_2",
    "c112", "c023", "c021", "z2_1", "pj_1", "c032", "z2b_2", "z4_0", "c123", "c121", "c012",
    "z2b_1", "z1_3", "c022", "z3_2", "pj_3", "z4b_0", "z3_1", "c122", "z1_4", "z3b_2", "z2_3",
    "z2_4", "z5_0", "pj_4", "nstart", "z3b_1", "z4_2", "z3_3", "z3_4", "z5b_0", "n030", "n010",
    "n130", "n110", "n103", "n101", "n003", "n001", "z4_1", "z4b_2", "n020", "n033", "n031", "n133",
    "n131", "n013", "n011", "n120", "n113", "n111", "n002", "n102", "z4_3", "n023", "n021", "z6_0",
    "n132", "n032", "n012", "z4_4", "z4b_1", "n123", "n121", "z7_0", "n112", "n022", "z5_2", "n122",
    "upd", "z5_3", "z5b_2", "z5_1", "z5_4", "z6_3", "z6_2", "z5b_1", "z7_3", "z7_2", "z6_4", "z6_1",
    "z7_4", "z7_1",
)


def remote(src, dst, send, recv, dev):
    return pltpu.make_async_remote_copy(
        src_ref=src, dst_ref=dst, send_sem=send, recv_sem=recv, device_id=dev, device_id_type=MESH
    )


class Gather:
    def __init__(self, buf, full, half, send_full, send_half, x, y):
        self.buf, self.full, self.half = buf, full, half
        self.send_full, self.send_half = send_full, send_half
        self.x, self.y = x, y
        self.rows = buf.shape[2] // 2
        self.sent = []

    def piece(self, g, u, v):
        dy, dx = (v, u) if g == 0 else (u, v)
        return lax.rem(self.y + dy, 4) * 4 + lax.rem(self.x + dx, 4)

    def device(self, g, axis, delta):
        along_x = (axis == 1) == (g == 0)
        if along_x:
            return {"dp": self.y * 4 + lax.rem(self.x + delta, 4)}
        return {"dp": lax.rem(self.y + delta, 4) * 4 + self.x}

    def send(self, g, axis, u, v, delta):
        p = self.piece(g, u, v)
        slot = 0 if axis == 1 else 1 + u
        ref = self.buf.at[g, p]
        copy = remote(
            ref, ref, self.send_full.at[g, slot, delta // 2], self.full.at[g, p],
            self.device(g, axis, delta),
        )
        copy.start()
        self.sent.append(copy)

    def relay(self, g, axis, u, v):
        off = u if axis == 1 else v
        delta, h = (3, 1) if off == 1 else (1, 0)
        p = self.piece(g, u, v)
        slot = 0 if axis == 1 else 1 + u
        ref = self.buf.at[g, p, pl.ds(h * self.rows, self.rows)]
        copy = remote(
            ref, ref, self.send_half.at[g, slot, h], self.half.at[g, p, h],
            self.device(g, axis, delta),
        )
        copy.start()
        self.sent.append(copy)

    def wait_full(self, g, u, v):
        p = self.piece(g, u, v)
        ref = self.buf.at[g, p]
        remote(
            ref, ref, self.send_full.at[g, 0, 0], self.full.at[g, p], self.device(g, 1, 1)
        ).wait_recv()

    def wait_halves(self, g, u, v):
        p = self.piece(g, u, v)
        for h in (0, 1):
            ref = self.buf.at[g, p, pl.ds(h * self.rows, self.rows)]
            remote(
                ref, ref, self.send_half.at[g, 0, 0], self.half.at[g, p, h], self.device(g, 1, 1)
            ).wait_recv()

    def start(self):
        for axis in (1, 2):
            for g in (0, 1):
                for delta in (1, 3):
                    self.send(g, axis, 0, 0, delta)

    def step(self, g, u, v):
        if 2 in (u if v == 0 else v, v):
            self.wait_halves(g, u, v)
        else:
            self.wait_full(g, u, v)
            self.relay(g, 1 if v == 0 else 2, u, v)
        if v == 0:
            for delta in (1, 3):
                self.send(g, 2, u, 0, delta)

    def drain(self):
        for copy in self.sent:
            copy.wait_send()


def pick(index, values):
    out = values[0]
    for i in range(1, len(values)):
        out = jnp.where(index == i, values[i], out)
    return out


def kernel(
    act_h, cot_h, w_h, basis_h, m1_h, m2_h, step_s,
    ig_h, norm_h, fn_h, sn_h,
    act, basis, w, m1, m2, cot, ct_own, ct, norm, acc, tmp, kept, sib_s, sib_r,
    a_s, a_r, b_s, b_r, out, ig,
    load_sem, ct_send, ct_recv, c_full, c_half, c_sf, c_sh, n_full, n_half, n_sf, n_sh,
    sib_ss, sib_rs, za_s, za_r, zb_s, zb_r, zc_s, zc_r, zd_s, zd_r, ze_s, ze_r, store_sem,
):
    dp = lax.axis_index("dp")
    tensor = lax.axis_index("tensor")
    y, x = lax.div(dp, 4), lax.rem(dp, 4)
    z, c = lax.div(tensor, 2), lax.rem(tensor, 2)
    oc = 1 - c
    up = 1 - 2 * c
    r0, q0 = lax.rem(z, 4), lax.div(z, 4)

    def along_z(delta):
        return {"tensor": lax.rem(z + delta + 16, 16) * 2 + c}

    def kind(delta):
        return lax.rem(z + delta + 4, 4)

    sibling = {"tensor": z * 2 + oc}

    loads = [
        pltpu.make_async_copy(cot_h.at[0], cot.at[0, dp], load_sem.at[0]),
        pltpu.make_async_copy(cot_h.at[1], cot.at[1, dp], load_sem.at[1]),
        pltpu.make_async_copy(act_h, act, load_sem.at[2]),
        pltpu.make_async_copy(basis_h, basis, load_sem.at[3]),
        pltpu.make_async_copy(w_h, w, load_sem.at[4]),
        pltpu.make_async_copy(m1_h, m1, load_sem.at[5]),
        pltpu.make_async_copy(m2_h, m2, load_sem.at[6]),
    ]
    for load in loads:
        load.start()

    barrier = pltpu.get_barrier_semaphore()

    def greet(d, carry):
        pl.semaphore_signal(
            barrier, inc=1, device_id={"dp": lax.rem(dp + d, 16)}, device_id_type=MESH
        )
        return carry

    lax.fori_loop(1, 16, greet, 0)
    for delta in (1, -1, 2, -2, 4, -4, 8):
        pl.semaphore_signal(barrier, inc=1, device_id=along_z(delta), device_id_type=MESH)
    pl.semaphore_signal(barrier, inc=1, device_id=sibling, device_id_type=MESH)
    pl.semaphore_wait(barrier, 23)

    gather = Gather(cot, c_full, c_half, c_sf, c_sh, x, y)
    ngather = Gather(norm, n_full, n_half, n_sf, n_sh, x, y)
    sends = []
    stores = []

    def cstart():
        loads[0].wait()
        loads[1].wait()
        gather.start()

    def coords():
        loads[2].wait()
        loads[3].wait()

        def coord_step(i, total):
            cols = pl.ds(pl.multiple_of(i * 1024, 1024), 1024)
            return total + jnp.dot(act[:, cols], basis[cols, :], preferred_element_type=F32)

        total = lax.fori_loop(0, 8, coord_step, jnp.zeros((128, 512), F32))
        ct_own[...] = total.T.astype(BF16)

    def ct_copy(d):
        to = lax.rem(dp + d, 16)
        rows = pl.ds(pl.multiple_of(to * 32, 32), 32)
        return remote(ct_own.at[rows], ct.at[dp], ct_send.at[d], ct_recv.at[dp], {"dp": to})

    def ct_go():
        def ct_start(d, carry):
            ct_copy(d).start()
            return carry

        lax.fori_loop(1, 16, ct_start, 0)
        ct[dp] = ct_own[pl.ds(pl.multiple_of(dp * 32, 32), 32), :]

    def ct_take():
        def ct_wait(d, carry):
            s = lax.rem(dp + d, 16)
            remote(ct.at[s], ct.at[s], ct_send.at[d], ct_recv.at[s], {"dp": s}).wait_recv()
            return carry

        lax.fori_loop(1, 16, ct_wait, 0)
        acc[...] = jnp.zeros_like(acc)

    def places(k):
        return [lax.rem(y + dy, 4) * 4 + lax.rem(x + dx, 4) for dy, dx in ROUNDS[k]]

    def first(k):
        return sum(len(r) for r in ROUNDS[:k])

    def project(k):
        spots = places(k)

        def step(i, carry):
            p = pick(i, spots)
            for g in (0, 1):
                acc[g] += jnp.dot(ct[p], cot[g, p], preferred_element_type=F32)
            return carry

        lax.fori_loop(0, len(spots), step, 0)

    def send(src, dst, ss, rs, dev):
        copy = remote(src, dst, ss, rs, dev)
        copy.start()
        sends.append(copy)

    def take(ref, ss, rs):
        remote(ref, ref, ss, rs, sibling).wait_recv()

    def span(k):
        return pl.ds(first(k) * 64, len(ROUNDS[k]) * 64)

    def bspan(k):
        return pl.ds(first(k) * 16, len(ROUNDS[k]) * 16)

    def chunk(k, steps):
        n = len(ROUNDS[k])
        q = lax.rem(q0 + steps + 4, 4)
        return pl.ds(pl.multiple_of(first(k) * 64 + q * (16 * n), 16), 16 * n)

    def z1(k):
        spots = places(k)

        def step(i, carry):
            p = pick(i, spots)
            part = lax.dot_general(
                cot[0, p], w[0], (((1,), (1,)), ((), ())), preferred_element_type=F32
            )
            part += lax.dot_general(
                cot[1, p], w[1], (((1,), (1,)), ((), ())), preferred_element_type=F32
            )
            tmp[0] = part[:64]
            tmp[1] = part[64:]
            rows = pl.ds(pl.multiple_of((first(k) + i) * 64, 64), 64)
            for r in range(4):
                kept[r, rows] = tmp[c, :, r * 128 : (r + 1) * 128]
                sib_s[r, rows] = tmp[oc, :, r * 128 : (r + 1) * 128].astype(BF16)
            return carry

        if k == 0:
            loads[4].wait()
        lax.fori_loop(0, len(spots), step, 0)
        rows = span(k)
        send(sib_s.at[:, rows], sib_r.at[:, rows], sib_ss.at[k], sib_rs.at[k], sibling)

    def z2(k):
        rows = span(k)
        take(sib_r.at[:, rows], sib_ss.at[k], sib_rs.at[k])

        def step(r, carry):
            kept[r, rows] = kept[r, rows] + sib_r[r, rows].astype(F32)
            return carry

        lax.fori_loop(0, 4, step, 0)
        moves = ((2 * up, up), (-up, -up)) if RELAYED[k] else ((up, up), (-up, -up), (2 * up, 2 * up))
        for i, (what, where) in enumerate(moves):
            a_s[i, rows] = kept[kind(what), rows].astype(BF16)
            send(
                a_s.at[i, rows], a_r.at[i, rows], za_s.at[k, i], za_r.at[k, i], along_z(where)
            )

    def z2b(k):
        rows = span(k)
        take(a_r.at[0, rows], za_s.at[k, 0], za_r.at[k, 0])
        a_s[2, rows] = (kept[kind(up), rows] + a_r[0, rows].astype(F32)).astype(BF16)
        send(a_s.at[2, rows], a_r.at[2, rows], za_s.at[k, 2], za_r.at[k, 2], along_z(up))

    def z3(k):
        rows, brows = span(k), bspan(k)
        total = kept[r0, rows]
        for i in (1, 2) if RELAYED[k] else (0, 1, 2):
            take(a_r.at[i, rows], za_s.at[k, i], za_r.at[k, i])
            total = total + a_r[i, rows].astype(F32)
        kept[r0, rows] = total
        moves = (
            ((2, 4 * up), (-up, -4 * up)) if RELAYED[k] else ((up, 4 * up), (-up, -4 * up), (2, 8))
        )
        for i, (what, where) in enumerate(moves):
            b_s[i, brows] = kept[r0, chunk(k, what)].astype(BF16)
            send(
                b_s.at[i, brows], b_r.at[i, brows], zb_s.at[k, i], zb_r.at[k, i], along_z(where)
            )

    def z3b(k):
        brows = bspan(k)
        take(b_r.at[0, brows], zb_s.at[k, 0], zb_r.at[k, 0])
        b_s[2, brows] = (kept[r0, chunk(k, up)] + b_r[0, brows].astype(F32)).astype(BF16)
        send(b_s.at[2, brows], b_r.at[2, brows], zb_s.at[k, 2], zb_r.at[k, 2], along_z(4 * up))

    def z4(k):
        brows = bspan(k)
        total = kept[r0, chunk(k, 0)]
        for i in (1, 2) if RELAYED[k] else (0, 1, 2):
            take(b_r.at[i, brows], zb_s.at[k, i], zb_r.at[k, i])
            total = total + b_r[i, brows].astype(F32)
        out[c, r0, chunk(k, 0)] = total.astype(BF16)
        ref = out.at[c, r0, chunk(k, 0)]
        for i, where in enumerate((4 * up, -4 * up) if RELAYED[k] else (4 * up, -4 * up, 8)):
            send(ref, ref, zc_s.at[k, i], zc_r.at[k, i], along_z(where))

    def z4b(k):
        ref = out.at[c, r0, chunk(k, -up)]
        take(ref, zc_s.at[k, 0], zc_r.at[k, 0])
        send(ref, ref, zc_s.at[k, 2], zc_r.at[k, 2], along_z(4 * up))

    def z5(k):
        for i, steps in enumerate((-up, up, 2)):
            if i > 0 or not RELAYED[k]:
                take(out.at[c, r0, chunk(k, steps)], zc_s.at[k, i], zc_r.at[k, i])
        ref = out.at[c, r0, span(k)]
        for i, where in enumerate((up, -up) if RELAYED[k] else (up, -up, 2 * up)):
            send(ref, ref, zd_s.at[k, i], zd_r.at[k, i], along_z(where))

    def z5b(k):
        ref = out.at[c, kind(-up), span(k)]
        take(ref, zd_s.at[k, 0], zd_r.at[k, 0])
        send(ref, ref, zd_s.at[k, 2], zd_r.at[k, 2], along_z(up))

    def z6(k):
        rows = span(k)
        for i, steps in enumerate((-up, up, 2)):
            if i > 0 or not RELAYED[k]:
                take(out.at[c, kind(steps), rows], zd_s.at[k, i], zd_r.at[k, i])
        ref = out.at[c, :, rows]
        send(ref, ref, ze_s.at[k], ze_r.at[k], sibling)

    def ig_copy(k, i):
        rows = pl.ds(pl.multiple_of(pick(i, places(k)) * 128, 128), 128)
        return pltpu.make_async_copy(ig.at[rows], ig_h.at[rows], store_sem.at[first(k) + i])

    def z7(k):
        take(out.at[oc, :, span(k)], ze_s.at[k], ze_r.at[k])
        spots = places(k)

        def step(i, carry):
            p = pick(i, spots)
            source = pl.ds(pl.multiple_of((first(k) + i) * 64, 64), 64)
            for half in range(2):
                rows = pl.ds(pl.multiple_of(p * 128 + half * 64, 64), 64)
                for r in range(4):
                    ig[rows, r * 128 : (r + 1) * 128] = out[half, r, source]
            ig_copy(k, i).start()
            return carry

        lax.fori_loop(0, len(spots), step, 0)

    def nstart():
        loads[5].wait()
        loads[6].wait()
        step_value = jnp.full((1, 1), step_s[0].astype(F32), F32)
        first_fix = 1.0 - jnp.exp(step_value * math.log(beta_one))
        second_fix = 1.0 - jnp.exp(step_value * math.log(beta_two))
        for g in (0, 1):
            projected = acc[g]
            first_new = beta_one * m1[g] + (1.0 - beta_one) * projected
            second_new = beta_two * m2[g] + (1.0 - beta_two) * projected * projected
            m1[g] = first_new
            m2[g] = second_new
            norm[g, dp] = (
                first_new / first_fix / (jnp.sqrt(second_new / second_fix) + adam_eps)
            ).astype(BF16)
        ngather.start()
        for ref, dst, i in ((m1, fn_h, 5), (m2, sn_h, 6)):
            store = pltpu.make_async_copy(ref, dst, load_sem.at[i])
            store.start()
            stores.append(store)

    def nstore():
        store = pltpu.make_async_copy(norm, norm_h, load_sem.at[0])
        store.start()
        stores.append(store)

    steps = dict(
        cstart=cstart, coords=coords, ct=ct_go, ctw=ct_take, nstart=nstart, upd=nstore,
        pj=project, z1=z1, z2=z2, z2b=z2b, z3=z3, z3b=z3b, z4=z4, z4b=z4b, z5=z5, z5b=z5b,
        z6=z6, z7=z7,
    )
    for name in ORDER:
        if name in steps:
            steps[name]()
        elif "_" in name:
            step, k = name.split("_")
            steps[step](int(k))
        else:
            g, u, v = (int(digit) for digit in name[1:])
            (gather if name[0] == "c" else ngather).step(g, u, v)

    gather.drain()
    ngather.drain()
    for copy in sends:
        copy.wait_send()

    def ct_drain(d, carry):
        ct_copy(d).wait_send()
        return carry

    lax.fori_loop(1, 16, ct_drain, 0)
    for store in stores:
        store.wait()
    for k in range(len(ROUNDS)):

        def stored(i, carry, k=k):
            ig_copy(k, i).wait()
            return carry

        lax.fori_loop(0, len(ROUNDS[k]), stored, 0)


def finish(ig_i, norm_i, basis_h, m1_i, m2_i, ig_o, upd_o, fn_o, sn_o, ig, norm, rows, upd, m1, m2, sem):
    dp = lax.axis_index("dp")
    pairs = []

    def move(i, src, ref, dst):
        pairs.append(
            (pltpu.make_async_copy(src, ref, sem.at[0, i]), pltpu.make_async_copy(ref, dst, sem.at[1, i]))
        )

    own = pltpu.make_async_copy(
        basis_h.at[pl.ds(pl.multiple_of(dp * 512, 512), 512)], rows, sem.at[0, 0]
    )
    halves = [
        (
            pltpu.make_async_copy(norm_i.at[g], norm.at[g], sem.at[0, 1 + g]),
            pltpu.make_async_copy(upd.at[g], upd_o.at[g], sem.at[1, 1 + g]),
        )
        for g in (0, 1)
    ]
    for j in range(4):
        part = pl.ds(j * 512, 512)
        move(3 + j, ig_i.at[part], ig.at[part], ig_o.at[part])
    move(7, m1_i, m1, fn_o)
    move(8, m2_i, m2, sn_o)
    own.start()
    halves[0][0].start()
    halves[1][0].start()
    for load, store in pairs:
        load.start()
    own.wait()
    for g, (load, store) in enumerate(halves):
        load.wait()
        upd[g] = jnp.dot(
            rows[...], norm[g].reshape(512, 896), preferred_element_type=F32
        ).astype(BF16)
        store.start()
        for pair in pairs[3 * g : 3 * g + 3]:
            pair[0].wait()
            pair[1].start()
    for load, store in halves + pairs:
        store.wait()


def local(activations, cotangent, weights, proj_basis, first_moment, second_moment, step_number):
    any_spec = pl.BlockSpec(memory_space=pl.ANY)
    dma = pltpu.SemaphoreType.DMA
    rounds = len(ROUNDS)
    moment = jax.ShapeDtypeStruct((2, 32, 896), F32)
    grad, norm, first_new, second_new = pl.pallas_call(
        kernel,
        out_shape=(
            jax.ShapeDtypeStruct((2048, 512), BF16),
            jax.ShapeDtypeStruct((2, 16, 32, 896), BF16),
            moment,
            moment,
        ),
        in_specs=[any_spec] * 6 + [pl.BlockSpec(memory_space=pltpu.SMEM)],
        out_specs=[any_spec] * 4,
        scratch_shapes=[
            pltpu.VMEM((128, 8192), BF16),
            pltpu.VMEM((8192, 512), BF16),
            pltpu.VMEM((2, 512, 896), BF16),
            pltpu.VMEM((2, 32, 896), F32),
            pltpu.VMEM((2, 32, 896), F32),
            pltpu.VMEM((2, 16, 128, 896), BF16),
            pltpu.VMEM((512, 128), BF16),
            pltpu.VMEM((16, 32, 128), BF16),
            pltpu.VMEM((2, 16, 32, 896), BF16),
            pltpu.VMEM((2, 32, 896), F32),
            pltpu.VMEM((2, 64, 512), F32),
            pltpu.VMEM((4, 1024, 128), F32),
            pltpu.VMEM((4, 1024, 128), BF16),
            pltpu.VMEM((4, 1024, 128), BF16),
            pltpu.VMEM((3, 1024, 128), BF16),
            pltpu.VMEM((3, 1024, 128), BF16),
            pltpu.VMEM((3, 256, 128), BF16),
            pltpu.VMEM((3, 256, 128), BF16),
            pltpu.VMEM((2, 4, 1024, 128), BF16),
            pltpu.VMEM((2048, 512), BF16),
            dma((7,)),
            dma((16,)), dma((16,)),
            dma((2, 16)), dma((2, 16, 2)), dma((2, 5, 2)), dma((2, 5, 2)),
            dma((2, 16)), dma((2, 16, 2)), dma((2, 5, 2)), dma((2, 5, 2)),
            dma((rounds,)), dma((rounds,)),
            dma((rounds, 3)), dma((rounds, 3)),
            dma((rounds, 3)), dma((rounds, 3)),
            dma((rounds, 3)), dma((rounds, 3)),
            dma((rounds, 3)), dma((rounds, 3)),
            dma((rounds,)), dma((rounds,)),
            dma((16,)),
        ],
        compiler_params=pltpu.CompilerParams(
            collective_id=0, has_side_effects=True, vmem_limit_bytes=60 << 20
        ),
        cost_estimate=pl.CostEstimate(
            flops=5_100_000_000, bytes_accessed=22_000_000, transcendentals=60_000
        ),
    )(activations, cotangent, weights, proj_basis, first_moment, second_moment, step_number)
    return pl.pallas_call(
        finish,
        out_shape=(
            jax.ShapeDtypeStruct((2048, 512), BF16),
            jax.ShapeDtypeStruct((2, 512, 896), BF16),
            moment,
            moment,
        ),
        in_specs=[any_spec] * 5,
        out_specs=[any_spec] * 4,
        scratch_shapes=[
            pltpu.VMEM((2048, 512), BF16),
            pltpu.VMEM((2, 16, 32, 896), BF16),
            pltpu.VMEM((512, 512), BF16),
            pltpu.VMEM((2, 512, 896), BF16),
            pltpu.VMEM((2, 32, 896), F32),
            pltpu.VMEM((2, 32, 896), F32),
            dma((2, 9)),
        ],
        compiler_params=pltpu.CompilerParams(vmem_limit_bytes=60 << 20),
        cost_estimate=pl.CostEstimate(
            flops=940_000_000, bytes_accessed=9_000_000, transcendentals=0
        ),
    )(grad, norm, proj_basis, first_new, second_new)


def solution(mesh):
    return jax.shard_map(
        local,
        mesh=mesh,
        in_specs=(
            P("dp", None),
            P(None, "dp", "tensor"),
            P(None, "dp", "tensor"),
            P(),
            P(None, "dp", "tensor"),
            P(None, "dp", "tensor"),
            P(),
        ),
        out_specs=(
            P(None, "dp"),
            P(None, "dp", "tensor"),
            P(None, "dp", "tensor"),
            P(None, "dp", "tensor"),
        ),
        check_vma=False,
    )
```

```python
import functools
import math

import jax
import jax.numpy as jnp
from jax import lax
from jax.experimental import pallas as pl
from jax.experimental.pallas import tpu as pltpu
from jax.sharding import PartitionSpec as P

MESH = pl.DeviceIdType.MESH
beta_one = 0.9
beta_two = 0.999
adam_eps = 1e-08

F32 = jnp.float32
BF16 = jnp.bfloat16

PARTNERS = (1, -1, 2, -2, 4, -4, 8)
ROUNDS = (
    ((0, 0), (0, 1), (0, 3), (1, 0), (3, 0)),
    ((0, 2), (2, 0), (3, 3)),
    ((3, 1), (1, 3), (1, 1)),
    ((3, 2), (1, 2)),
    ((2, 3), (2, 1)),
    ((2, 2),),
)
RELAYED = (True, True, True, False, False, False)
ORDER = (
    "cstart", "coords", "ct", "c030", "c010", "c130", "c110", "c103", "c101", "c003", "c001",
    "z1_0", "c020", "ctw", "pj_0", "c033", "c031", "z2_0", "c133", "c131", "c013", "c011", "z2b_0",
    "c113", "c111", "c120", "z1_2", "z3_0", "c102", "c002", "pj_2", "z2_2", "c132", "z1_1", "z3b_0",
    "c112", "c023", "c021", "pj_1", "z2b_2", "z2_1", "c032", "z1_3", "z4_0", "c123", "c121", "c012",
    "z3_2", "z2b_1", "pj_3", "z2_3", "c022", "z1_4", "pj_4", "c122", "z4b_0", "z3b_2", "z3_1",
    "z2_4", "z1_5", "z3_3", "pj_5", "nstart", "z5_0", "z3b_1", "z4_2", "z2_5", "z3_4", "n030",
    "n010", "n130", "n110", "n103", "n101", "n003", "n001", "z4_3", "z4_1", "n020", "n033", "n031",
    "z3_5", "n133", "n131", "n013", "n011", "z5b_0", "n120", "n113", "n111", "n002", "n102",
    "z4b_2", "z4_4", "n023", "n021", "n132", "n032", "z4b_1", "n012", "z5_3", "z6_0", "n123",
    "n121", "n112", "z4_5", "z5_2", "n022", "z7_0", "z5_1", "n122", "upd", "z5_4", "z6_3", "z5b_2",
    "z5b_1", "z7_3", "z5_5", "z6_4", "z6_2", "z6_1", "z7_4", "z6_5", "z7_2", "z7_1", "z7_5",
)


def remote(src, dst, send, recv, dev):
    return pltpu.make_async_remote_copy(
        src_ref=src, dst_ref=dst, send_sem=send, recv_sem=recv, device_id=dev, device_id_type=MESH
    )


class Gather:
    def __init__(self, buf, full, half, send_full, send_half, x, y):
        self.buf, self.full, self.half = buf, full, half
        self.send_full, self.send_half = send_full, send_half
        self.x, self.y = x, y
        self.rows = buf.shape[2] // 2
        self.sent = []

    def piece(self, g, u, v):
        dy, dx = (v, u) if g == 0 else (u, v)
        return lax.rem(self.y + dy, 4) * 4 + lax.rem(self.x + dx, 4)

    def device(self, g, axis, delta):
        along_x = (axis == 1) == (g == 0)
        if along_x:
            return {"dp": self.y * 4 + lax.rem(self.x + delta, 4)}
        return {"dp": lax.rem(self.y + delta, 4) * 4 + self.x}

    def send(self, g, axis, u, v, delta):
        p = self.piece(g, u, v)
        slot = 0 if axis == 1 else 1 + u
        ref = self.buf.at[g, p]
        copy = remote(
            ref, ref, self.send_full.at[g, slot, delta // 2], self.full.at[g, p],
            self.device(g, axis, delta),
        )
        copy.start()
        self.sent.append(copy)

    def relay(self, g, axis, u, v):
        off = u if axis == 1 else v
        delta, h = (3, 1) if off == 1 else (1, 0)
        p = self.piece(g, u, v)
        slot = 0 if axis == 1 else 1 + u
        ref = self.buf.at[g, p, pl.ds(h * self.rows, self.rows)]
        copy = remote(
            ref, ref, self.send_half.at[g, slot, h], self.half.at[g, p, h],
            self.device(g, axis, delta),
        )
        copy.start()
        self.sent.append(copy)

    def wait_full(self, g, u, v):
        p = self.piece(g, u, v)
        ref = self.buf.at[g, p]
        remote(
            ref, ref, self.send_full.at[g, 0, 0], self.full.at[g, p], self.device(g, 1, 1)
        ).wait_recv()

    def wait_halves(self, g, u, v):
        p = self.piece(g, u, v)
        for h in (0, 1):
            ref = self.buf.at[g, p, pl.ds(h * self.rows, self.rows)]
            remote(
                ref, ref, self.send_half.at[g, 0, 0], self.half.at[g, p, h], self.device(g, 1, 1)
            ).wait_recv()

    def start(self):
        for axis in (1, 2):
            for g in (0, 1):
                for delta in (1, 3):
                    self.send(g, axis, 0, 0, delta)

    def step(self, g, u, v):
        if 2 in (u if v == 0 else v, v):
            self.wait_halves(g, u, v)
        else:
            self.wait_full(g, u, v)
            self.relay(g, 1 if v == 0 else 2, u, v)
        if v == 0:
            for delta in (1, 3):
                self.send(g, 2, u, 0, delta)

    def drain(self):
        for copy in self.sent:
            copy.wait_send()


def pick(index, values):
    out = values[0]
    for i in range(1, len(values)):
        out = jnp.where(index == i, values[i], out)
    return out


def kernel(
    act_h, cot_h, w_h, basis_h, m1_h, m2_h, step_h,
    ig_h, norm_h, fn_h, sn_h,
    act, basis, w, m1, m2, cot, ct_own, ct, norm, acc, tmp, kept, sib_s, sib_r,
    a_s, a_r, b_s, b_r, out, ig,
    load_sem, ct_send, ct_recv, c_full, c_half, c_sf, c_sh, n_full, n_half, n_sf, n_sh,
    sib_ss, sib_rs, za_s, za_r, zb_s, zb_r, zc_s, zc_r, zd_s, zd_r, ze_s, ze_r, store_sem, z_ready, step_s,
):
    dp = lax.axis_index("dp")
    tensor = lax.axis_index("tensor")
    y, x = lax.div(dp, 4), lax.rem(dp, 4)
    z, c = lax.div(tensor, 2), lax.rem(tensor, 2)
    oc = 1 - c
    up = 1 - 2 * c
    r0, q0 = lax.rem(z, 4), lax.div(z, 4)

    def along_z(delta):
        return {"tensor": lax.rem(z + delta + 16, 16) * 2 + c}

    def kind(delta):
        return lax.rem(z + delta + 4, 4)

    sibling = {"tensor": z * 2 + oc}

    loads = [
        pltpu.make_async_copy(cot_h.at[0], cot.at[0, dp], load_sem.at[0]),
        pltpu.make_async_copy(cot_h.at[1], cot.at[1, dp], load_sem.at[1]),
        pltpu.make_async_copy(act_h, act, load_sem.at[2]),
        pltpu.make_async_copy(basis_h, basis, load_sem.at[3]),
        pltpu.make_async_copy(w_h, w, load_sem.at[4]),
        pltpu.make_async_copy(m1_h, m1, load_sem.at[5]),
        pltpu.make_async_copy(m2_h, m2, load_sem.at[6]),
        pltpu.make_async_copy(step_h, step_s, load_sem.at[7]),
    ]
    for load in loads:
        load.start()

    barrier = pltpu.get_barrier_semaphore()

    def greet(d, carry):
        pl.semaphore_signal(
            barrier, inc=1, device_id={"dp": lax.rem(dp + d, 16)}, device_id_type=MESH
        )
        return carry

    lax.fori_loop(1, 16, greet, 0)
    pl.semaphore_signal(barrier, inc=1, device_id=sibling, device_id_type=MESH)
    below = 0
    for delta in PARTNERS:
        above = lax.rem(z + delta + 16, 16) > z
        below = below + jnp.where(above, 0, 1)

        @pl.when(above)
        def _(delta=delta):
            pl.semaphore_signal(barrier, inc=1, device_id=along_z(delta), device_id_type=MESH)

    pl.semaphore_wait(barrier, 16 + below)
    for delta in PARTNERS:

        @pl.when(lax.rem(z + delta + 16, 16) < z)
        def _(delta=delta):
            pl.semaphore_signal(z_ready, inc=1, device_id=along_z(delta), device_id_type=MESH)

    gather = Gather(cot, c_full, c_half, c_sf, c_sh, x, y)
    ngather = Gather(norm, n_full, n_half, n_sf, n_sh, x, y)
    sends = []
    stores = []

    def cstart():
        loads[0].wait()
        loads[1].wait()
        gather.start()

    def coords():
        loads[2].wait()
        loads[3].wait()

        def coord_step(i, total):
            cols = pl.ds(pl.multiple_of(i * 1024, 1024), 1024)
            return total + jnp.dot(act[:, cols], basis[cols, :], preferred_element_type=F32)

        total = lax.fori_loop(0, 8, coord_step, jnp.zeros((128, 512), F32))
        ct_own[...] = total.T.astype(BF16)

    def ct_copy(d):
        to = lax.rem(dp + d, 16)
        rows = pl.ds(pl.multiple_of(to * 32, 32), 32)
        return remote(ct_own.at[rows], ct.at[dp], ct_send.at[d], ct_recv.at[dp], {"dp": to})

    def ct_go():
        def ct_start(d, carry):
            ct_copy(d).start()
            return carry

        lax.fori_loop(1, 16, ct_start, 0)
        ct[dp] = ct_own[pl.ds(pl.multiple_of(dp * 32, 32), 32), :]

    def ct_take():
        def ct_wait(d, carry):
            s = lax.rem(dp + d, 16)
            remote(ct.at[s], ct.at[s], ct_send.at[d], ct_recv.at[s], {"dp": s}).wait_recv()
            return carry

        lax.fori_loop(1, 16, ct_wait, 0)
        acc[...] = jnp.zeros_like(acc)

    def places(k):
        return [lax.rem(y + dy, 4) * 4 + lax.rem(x + dx, 4) for dy, dx in ROUNDS[k]]

    def first(k):
        return sum(len(r) for r in ROUNDS[:k])

    def project(k):
        spots = places(k)

        def step(i, carry):
            p = pick(i, spots)
            for g in (0, 1):
                acc[g] += jnp.dot(ct[p], cot[g, p], preferred_element_type=F32)
            return carry

        lax.fori_loop(0, len(spots), step, 0)

    def send(src, dst, ss, rs, dev):
        copy = remote(src, dst, ss, rs, dev)
        copy.start()
        sends.append(copy)

    def take(ref, ss, rs):
        remote(ref, ref, ss, rs, sibling).wait_recv()

    def span(k):
        return pl.ds(first(k) * 64, len(ROUNDS[k]) * 64)

    def bspan(k):
        return pl.ds(first(k) * 16, len(ROUNDS[k]) * 16)

    def chunk(k, steps):
        n = len(ROUNDS[k])
        q = lax.rem(q0 + steps + 4, 4)
        return pl.ds(pl.multiple_of(first(k) * 64 + q * (16 * n), 16), 16 * n)

    def z1(k):
        spots = places(k)

        def step(i, carry):
            p = pick(i, spots)
            part = lax.dot_general(
                cot[0, p], w[0], (((1,), (1,)), ((), ())), preferred_element_type=F32
            )
            part += lax.dot_general(
                cot[1, p], w[1], (((1,), (1,)), ((), ())), preferred_element_type=F32
            )
            tmp[0] = part[:64]
            tmp[1] = part[64:]
            rows = pl.ds(pl.multiple_of((first(k) + i) * 64, 64), 64)
            for r in range(4):
                kept[r, rows] = tmp[c, :, r * 128 : (r + 1) * 128]
                sib_s[r, rows] = tmp[oc, :, r * 128 : (r + 1) * 128].astype(BF16)
            return carry

        if k == 0:
            loads[4].wait()
        lax.fori_loop(0, len(spots), step, 0)
        rows = span(k)
        send(sib_s.at[:, rows], sib_r.at[:, rows], sib_ss.at[k], sib_rs.at[k], sibling)

    def z2(k):
        if ORDER.index(f"z2_{k}") == min(ORDER.index(f"z2_{j}") for j in range(len(ROUNDS))):

            @pl.when(below < len(PARTNERS))
            def _():
                pl.semaphore_wait(z_ready, len(PARTNERS) - below)

        rows = span(k)
        take(sib_r.at[:, rows], sib_ss.at[k], sib_rs.at[k])

        def step(r, carry):
            kept[r, rows] = kept[r, rows] + sib_r[r, rows].astype(F32)
            return carry

        lax.fori_loop(0, 4, step, 0)
        moves = ((2 * up, up), (-up, -up)) if RELAYED[k] else ((up, up), (-up, -up), (2 * up, 2 * up))
        for i, (what, where) in enumerate(moves):
            a_s[i, rows] = kept[kind(what), rows].astype(BF16)
            send(
                a_s.at[i, rows], a_r.at[i, rows], za_s.at[k, i], za_r.at[k, i], along_z(where)
            )

    def z2b(k):
        rows = span(k)
        take(a_r.at[0, rows], za_s.at[k, 0], za_r.at[k, 0])
        a_s[2, rows] = (kept[kind(up), rows] + a_r[0, rows].astype(F32)).astype(BF16)
        send(a_s.at[2, rows], a_r.at[2, rows], za_s.at[k, 2], za_r.at[k, 2], along_z(up))

    def z3(k):
        rows, brows = span(k), bspan(k)
        total = kept[r0, rows]
        for i in (1, 2) if RELAYED[k] else (0, 1, 2):
            take(a_r.at[i, rows], za_s.at[k, i], za_r.at[k, i])
            total = total + a_r[i, rows].astype(F32)
        kept[r0, rows] = total
        moves = (
            ((2, 4 * up), (-up, -4 * up)) if RELAYED[k] else ((up, 4 * up), (-up, -4 * up), (2, 8))
        )
        for i, (what, where) in enumerate(moves):
            b_s[i, brows] = kept[r0, chunk(k, what)].astype(BF16)
            send(
                b_s.at[i, brows], b_r.at[i, brows], zb_s.at[k, i], zb_r.at[k, i], along_z(where)
            )

    def z3b(k):
        brows = bspan(k)
        take(b_r.at[0, brows], zb_s.at[k, 0], zb_r.at[k, 0])
        b_s[2, brows] = (kept[r0, chunk(k, up)] + b_r[0, brows].astype(F32)).astype(BF16)
        send(b_s.at[2, brows], b_r.at[2, brows], zb_s.at[k, 2], zb_r.at[k, 2], along_z(4 * up))

    def z4(k):
        brows = bspan(k)
        total = kept[r0, chunk(k, 0)]
        for i in (1, 2) if RELAYED[k] else (0, 1, 2):
            take(b_r.at[i, brows], zb_s.at[k, i], zb_r.at[k, i])
            total = total + b_r[i, brows].astype(F32)
        out[c, r0, chunk(k, 0)] = total.astype(BF16)
        ref = out.at[c, r0, chunk(k, 0)]
        for i, where in enumerate((4 * up, -4 * up) if RELAYED[k] else (4 * up, -4 * up, 8)):
            send(ref, ref, zc_s.at[k, i], zc_r.at[k, i], along_z(where))

    def z4b(k):
        ref = out.at[c, r0, chunk(k, -up)]
        take(ref, zc_s.at[k, 0], zc_r.at[k, 0])
        send(ref, ref, zc_s.at[k, 2], zc_r.at[k, 2], along_z(4 * up))

    def z5(k):
        for i, steps in enumerate((-up, up, 2)):
            if i > 0 or not RELAYED[k]:
                take(out.at[c, r0, chunk(k, steps)], zc_s.at[k, i], zc_r.at[k, i])
        ref = out.at[c, r0, span(k)]
        for i, where in enumerate((up, -up) if RELAYED[k] else (up, -up, 2 * up)):
            send(ref, ref, zd_s.at[k, i], zd_r.at[k, i], along_z(where))

    def z5b(k):
        ref = out.at[c, kind(-up), span(k)]
        take(ref, zd_s.at[k, 0], zd_r.at[k, 0])
        send(ref, ref, zd_s.at[k, 2], zd_r.at[k, 2], along_z(up))

    def z6(k):
        rows = span(k)
        for i, steps in enumerate((-up, up, 2)):
            if i > 0 or not RELAYED[k]:
                take(out.at[c, kind(steps), rows], zd_s.at[k, i], zd_r.at[k, i])
        ref = out.at[c, :, rows]
        send(ref, ref, ze_s.at[k], ze_r.at[k], sibling)

    def ig_copy(k, i):
        rows = pl.ds(pl.multiple_of(pick(i, places(k)) * 128, 128), 128)
        return pltpu.make_async_copy(ig.at[rows], ig_h.at[rows], store_sem.at[first(k) + i])

    def z7(k):
        take(out.at[oc, :, span(k)], ze_s.at[k], ze_r.at[k])
        spots = places(k)

        def step(i, carry):
            p = pick(i, spots)
            source = pl.ds(pl.multiple_of((first(k) + i) * 64, 64), 64)
            for half in range(2):
                rows = pl.ds(pl.multiple_of(p * 128 + half * 64, 64), 64)
                for r in range(4):
                    ig[rows, r * 128 : (r + 1) * 128] = out[half, r, source]
            ig_copy(k, i).start()
            return carry

        lax.fori_loop(0, len(spots), step, 0)

    def nstart():
        loads[5].wait()
        loads[6].wait()
        loads[7].wait()
        step_value = jnp.full((1, 1), step_s[0].astype(F32), F32)
        first_fix = 1.0 - jnp.exp(step_value * math.log(beta_one))
        second_fix = 1.0 - jnp.exp(step_value * math.log(beta_two))
        for g in (0, 1):
            projected = acc[g]
            first_new = beta_one * m1[g] + (1.0 - beta_one) * projected
            second_new = beta_two * m2[g] + (1.0 - beta_two) * projected * projected
            m1[g] = first_new
            m2[g] = second_new
            norm[g, dp] = (
                first_new / first_fix / (jnp.sqrt(second_new / second_fix) + adam_eps)
            ).astype(BF16)
        ngather.start()
        for ref, dst, i in ((m1, fn_h, 5), (m2, sn_h, 6)):
            store = pltpu.make_async_copy(ref, dst, load_sem.at[i])
            store.start()
            stores.append(store)

    def nstore():
        store = pltpu.make_async_copy(norm, norm_h, load_sem.at[0])
        store.start()
        stores.append(store)

    steps = dict(
        cstart=cstart, coords=coords, ct=ct_go, ctw=ct_take, nstart=nstart, upd=nstore,
        pj=project, z1=z1, z2=z2, z2b=z2b, z3=z3, z3b=z3b, z4=z4, z4b=z4b, z5=z5, z5b=z5b,
        z6=z6, z7=z7,
    )
    for name in ORDER:
        if name in steps:
            steps[name]()
        elif "_" in name:
            step, k = name.split("_")
            steps[step](int(k))
        else:
            g, u, v = (int(digit) for digit in name[1:])
            (gather if name[0] == "c" else ngather).step(g, u, v)

    gather.drain()
    ngather.drain()
    for copy in sends:
        copy.wait_send()

    def ct_drain(d, carry):
        ct_copy(d).wait_send()
        return carry

    lax.fori_loop(1, 16, ct_drain, 0)
    for store in stores:
        store.wait()
    for k in range(len(ROUNDS)):

        def stored(i, carry, k=k):
            ig_copy(k, i).wait()
            return carry

        lax.fori_loop(0, len(ROUNDS[k]), stored, 0)


def finish(ig_i, norm_i, basis_h, m1_i, m2_i, ig_o, upd_o, fn_o, sn_o, ig, norm, rows, upd, m1, m2, sem):
    dp = lax.axis_index("dp")
    pairs = []

    def move(i, src, ref, dst):
        pairs.append(
            (pltpu.make_async_copy(src, ref, sem.at[0, i]), pltpu.make_async_copy(ref, dst, sem.at[1, i]))
        )

    own = pltpu.make_async_copy(
        basis_h.at[pl.ds(pl.multiple_of(dp * 512, 512), 512)], rows, sem.at[0, 0]
    )
    halves = [
        (
            pltpu.make_async_copy(norm_i.at[g], norm.at[g], sem.at[0, 1 + g]),
            pltpu.make_async_copy(upd.at[g], upd_o.at[g], sem.at[1, 1 + g]),
        )
        for g in (0, 1)
    ]
    for j in range(4):
        part = pl.ds(j * 512, 512)
        move(3 + j, ig_i.at[part], ig.at[part], ig_o.at[part])
    move(7, m1_i, m1, fn_o)
    move(8, m2_i, m2, sn_o)
    own.start()
    halves[0][0].start()
    for load, store in pairs[:2]:
        load.start()
    halves[1][0].start()
    for load, store in pairs[2:]:
        load.start()
    own.wait()
    for g, (load, store) in enumerate(halves):
        load.wait()
        upd[g] = jnp.dot(
            rows[...], norm[g].reshape(512, 896), preferred_element_type=F32
        ).astype(BF16)
        store.start()
        for pair in pairs[2 * g : 2 * g + 2] if g == 0 else pairs[2:]:
            pair[0].wait()
            pair[1].start()
    for load, store in halves + pairs:
        store.wait()


def local(activations, cotangent, weights, proj_basis, first_moment, second_moment, step_number):
    any_spec = pl.BlockSpec(memory_space=pl.ANY)
    dma = pltpu.SemaphoreType.DMA
    rounds = len(ROUNDS)
    moment = jax.ShapeDtypeStruct((2, 32, 896), F32)
    grad, norm, first_new, second_new = pl.pallas_call(
        kernel,
        out_shape=(
            jax.ShapeDtypeStruct((2048, 512), BF16),
            jax.ShapeDtypeStruct((2, 16, 32, 896), BF16),
            moment,
            moment,
        ),
        in_specs=[any_spec] * 6 + [pl.BlockSpec(memory_space=pltpu.HBM)],
        out_specs=[any_spec] * 4,
        scratch_shapes=[
            pltpu.VMEM((128, 8192), BF16),
            pltpu.VMEM((8192, 512), BF16),
            pltpu.VMEM((2, 512, 896), BF16),
            pltpu.VMEM((2, 32, 896), F32),
            pltpu.VMEM((2, 32, 896), F32),
            pltpu.VMEM((2, 16, 128, 896), BF16),
            pltpu.VMEM((512, 128), BF16),
            pltpu.VMEM((16, 32, 128), BF16),
            pltpu.VMEM((2, 16, 32, 896), BF16),
            pltpu.VMEM((2, 32, 896), F32),
            pltpu.VMEM((2, 64, 512), F32),
            pltpu.VMEM((4, 1024, 128), F32),
            pltpu.VMEM((4, 1024, 128), BF16),
            pltpu.VMEM((4, 1024, 128), BF16),
            pltpu.VMEM((3, 1024, 128), BF16),
            pltpu.VMEM((3, 1024, 128), BF16),
            pltpu.VMEM((3, 256, 128), BF16),
            pltpu.VMEM((3, 256, 128), BF16),
            pltpu.VMEM((2, 4, 1024, 128), BF16),
            pltpu.VMEM((2048, 512), BF16),
            dma((8,)),
            dma((16,)), dma((16,)),
            dma((2, 16)), dma((2, 16, 2)), dma((2, 5, 2)), dma((2, 5, 2)),
            dma((2, 16)), dma((2, 16, 2)), dma((2, 5, 2)), dma((2, 5, 2)),
            dma((rounds,)), dma((rounds,)),
            dma((rounds, 3)), dma((rounds, 3)),
            dma((rounds, 3)), dma((rounds, 3)),
            dma((rounds, 3)), dma((rounds, 3)),
            dma((rounds, 3)), dma((rounds, 3)),
            dma((rounds,)), dma((rounds,)),
            dma((16,)),
            pltpu.SemaphoreType.REGULAR,
            pltpu.SMEM((1,), jnp.int32),
        ],
        compiler_params=pltpu.CompilerParams(
            collective_id=0, has_side_effects=True, vmem_limit_bytes=60 << 20
        ),
        cost_estimate=pl.CostEstimate(
            flops=5_100_000_000, bytes_accessed=22_000_000, transcendentals=60_000
        ),
    )(activations, cotangent, weights, proj_basis, first_moment, second_moment, step_number)
    return pl.pallas_call(
        finish,
        out_shape=(
            jax.ShapeDtypeStruct((2048, 512), BF16),
            jax.ShapeDtypeStruct((2, 512, 896), BF16),
            moment,
            moment,
        ),
        in_specs=[any_spec] * 5,
        out_specs=[any_spec] * 4,
        scratch_shapes=[
            pltpu.VMEM((2048, 512), BF16),
            pltpu.VMEM((2, 16, 32, 896), BF16),
            pltpu.VMEM((512, 512), BF16),
            pltpu.VMEM((2, 512, 896), BF16),
            pltpu.VMEM((2, 32, 896), F32),
            pltpu.VMEM((2, 32, 896), F32),
            dma((2, 9)),
        ],
        compiler_params=pltpu.CompilerParams(vmem_limit_bytes=60 << 20),
        cost_estimate=pl.CostEstimate(
            flops=940_000_000, bytes_accessed=9_000_000, transcendentals=0
        ),
    )(grad, norm, proj_basis, first_new, second_new)


def solution(mesh):
    return jax.shard_map(
        local,
        mesh=mesh,
        in_specs=(
            P("dp", None),
            P(None, "dp", "tensor"),
            P(None, "dp", "tensor"),
            P(),
            P(None, "dp", "tensor"),
            P(None, "dp", "tensor"),
            P(),
        ),
        out_specs=(
            P(None, "dp"),
            P(None, "dp", "tensor"),
            P(None, "dp", "tensor"),
            P(None, "dp", "tensor"),
        ),
        check_vma=False,
    )
```

```python
import functools
import math

import jax
import jax.numpy as jnp
from jax import lax
from jax.experimental import pallas as pl
from jax.experimental.pallas import tpu as pltpu
from jax.sharding import PartitionSpec as P

MESH = pl.DeviceIdType.MESH
beta_one = 0.9
beta_two = 0.999
adam_eps = 1e-08

F32 = jnp.float32
KERNEL_MIB = 57
BF16 = jnp.bfloat16

PARTNERS = (1, -1, 2, -2, 4, -4, 8)
ROUNDS = (
    ((0, 0), (0, 1), (0, 3), (1, 0), (3, 0)),
    ((0, 2), (2, 0), (3, 3)),
    ((3, 1), (1, 3), (1, 1)),
    ((3, 2), (1, 2)),
    ((2, 3), (2, 1)),
    ((2, 2),),
)
RELAYED = (True, True, True, False, False, False)
ORDER = (
    "cstart", "coords", "ct", "c030", "c010", "c130", "c110", "c103", "c101", "c003", "c001",
    "z1_0", "c020", "ctw", "pj_0", "c033", "c031", "z2_0", "c133", "c131", "c013", "c011", "z2b_0",
    "c113", "c111", "c120", "z1_2", "z3_0", "c102", "c002", "pj_2", "z2_2", "c132", "z1_1", "z3b_0",
    "c112", "c023", "c021", "pj_1", "z2b_2", "z2_1", "c032", "z1_3", "z4_0", "c123", "c121", "c012",
    "z3_2", "z2b_1", "pj_3", "z2_3", "c022", "z1_4", "pj_4", "c122", "z4b_0", "z3b_2", "z3_1",
    "z2_4", "z1_5", "z3_3", "pj_5", "nstart", "z5_0", "z3b_1", "z4_2", "z2_5", "z3_4", "n030",
    "n010", "n130", "n110", "n103", "n101", "n003", "n001", "z4_3", "z4_1", "n020", "n033", "n031",
    "z3_5", "n133", "n131", "n013", "n011", "z5b_0", "n120", "n113", "n111", "n002", "n102",
    "z4b_2", "z4_4", "n023", "n021", "n132", "n032", "z4b_1", "n012", "z5_3", "z6_0", "n123",
    "n121", "n112", "z4_5", "z5_2", "n022", "z7_0", "z5_1", "n122", "upd", "z5_4", "z6_3", "z5b_2",
    "z5b_1", "z7_3", "z5_5", "z6_4", "z6_2", "z6_1", "z7_4", "z6_5", "z7_2", "z7_1", "z7_5",
)


def remote(src, dst, send, recv, dev):
    return pltpu.make_async_remote_copy(
        src_ref=src, dst_ref=dst, send_sem=send, recv_sem=recv, device_id=dev, device_id_type=MESH
    )


class Gather:
    def __init__(self, buf, full, half, send_full, send_half, x, y):
        self.buf, self.full, self.half = buf, full, half
        self.send_full, self.send_half = send_full, send_half
        self.x, self.y = x, y
        self.rows = buf.shape[2] // 2
        self.sent = []

    def piece(self, g, u, v):
        dy, dx = (v, u) if g == 0 else (u, v)
        return lax.rem(self.y + dy, 4) * 4 + lax.rem(self.x + dx, 4)

    def device(self, g, axis, delta):
        along_x = (axis == 1) == (g == 0)
        if along_x:
            return {"dp": self.y * 4 + lax.rem(self.x + delta, 4)}
        return {"dp": lax.rem(self.y + delta, 4) * 4 + self.x}

    def send(self, g, axis, u, v, delta):
        p = self.piece(g, u, v)
        slot = 0 if axis == 1 else 1 + u
        ref = self.buf.at[g, p]
        copy = remote(
            ref, ref, self.send_full.at[g, slot, delta // 2], self.full.at[g, p],
            self.device(g, axis, delta),
        )
        copy.start()
        self.sent.append(copy)

    def relay(self, g, axis, u, v):
        off = u if axis == 1 else v
        delta, h = (3, 1) if off == 1 else (1, 0)
        p = self.piece(g, u, v)
        slot = 0 if axis == 1 else 1 + u
        ref = self.buf.at[g, p, pl.ds(h * self.rows, self.rows)]
        copy = remote(
            ref, ref, self.send_half.at[g, slot, h], self.half.at[g, p, h],
            self.device(g, axis, delta),
        )
        copy.start()
        self.sent.append(copy)

    def wait_full(self, g, u, v):
        p = self.piece(g, u, v)
        ref = self.buf.at[g, p]
        remote(
            ref, ref, self.send_full.at[g, 0, 0], self.full.at[g, p], self.device(g, 1, 1)
        ).wait_recv()

    def wait_halves(self, g, u, v):
        p = self.piece(g, u, v)
        for h in (0, 1):
            ref = self.buf.at[g, p, pl.ds(h * self.rows, self.rows)]
            remote(
                ref, ref, self.send_half.at[g, 0, 0], self.half.at[g, p, h], self.device(g, 1, 1)
            ).wait_recv()

    def start(self):
        for axis in (1, 2):
            for g in (0, 1):
                for delta in (1, 3):
                    self.send(g, axis, 0, 0, delta)

    def step(self, g, u, v):
        if 2 in (u if v == 0 else v, v):
            self.wait_halves(g, u, v)
        else:
            self.wait_full(g, u, v)
            self.relay(g, 1 if v == 0 else 2, u, v)
        if v == 0:
            for delta in (1, 3):
                self.send(g, 2, u, 0, delta)

    def drain(self):
        for copy in self.sent:
            copy.wait_send()


def pick(index, values):
    out = values[0]
    for i in range(1, len(values)):
        out = jnp.where(index == i, values[i], out)
    return out


def kernel(
    act_h, cot_h, w_h, basis_h, m1_h, m2_h, step_h,
    ig_h, upd_h, fn_h, sn_h,
    act, basis, w, m1, m2, cot, ct_own, ct, norm, acc, tmp, kept, sib_s, sib_r,
    a_s, a_r, b_s, b_r, out, ig, upd,
    load_sem, ct_send, ct_recv, c_full, c_half, c_sf, c_sh, n_full, n_half, n_sf, n_sh,
    sib_ss, sib_rs, za_s, za_r, zb_s, zb_r, zc_s, zc_r, zd_s, zd_r, ze_s, ze_r, store_sem, z_ready, step_s,
):
    dp = lax.axis_index("dp")
    tensor = lax.axis_index("tensor")
    y, x = lax.div(dp, 4), lax.rem(dp, 4)
    z, c = lax.div(tensor, 2), lax.rem(tensor, 2)
    oc = 1 - c
    up = 1 - 2 * c
    r0, q0 = lax.rem(z, 4), lax.div(z, 4)

    def along_z(delta):
        return {"tensor": lax.rem(z + delta + 16, 16) * 2 + c}

    def kind(delta):
        return lax.rem(z + delta + 4, 4)

    sibling = {"tensor": z * 2 + oc}

    loads = [
        pltpu.make_async_copy(cot_h.at[0], cot.at[0, dp], load_sem.at[0]),
        pltpu.make_async_copy(cot_h.at[1], cot.at[1, dp], load_sem.at[1]),
        pltpu.make_async_copy(act_h, act, load_sem.at[2]),
        pltpu.make_async_copy(basis_h, basis, load_sem.at[3]),
        pltpu.make_async_copy(w_h, w, load_sem.at[4]),
        pltpu.make_async_copy(m1_h, m1, load_sem.at[5]),
        pltpu.make_async_copy(m2_h, m2, load_sem.at[6]),
        pltpu.make_async_copy(step_h, step_s, load_sem.at[7]),
    ]
    for load in loads:
        load.start()

    barrier = pltpu.get_barrier_semaphore()

    def greet(d, carry):
        pl.semaphore_signal(
            barrier, inc=1, device_id={"dp": lax.rem(dp + d, 16)}, device_id_type=MESH
        )
        return carry

    lax.fori_loop(1, 16, greet, 0)
    pl.semaphore_signal(barrier, inc=1, device_id=sibling, device_id_type=MESH)
    below = 0
    for delta in PARTNERS:
        above = lax.rem(z + delta + 16, 16) > z
        below = below + jnp.where(above, 0, 1)

        @pl.when(above)
        def _(delta=delta):
            pl.semaphore_signal(barrier, inc=1, device_id=along_z(delta), device_id_type=MESH)

    pl.semaphore_wait(barrier, 16 + below)
    for delta in PARTNERS:

        @pl.when(lax.rem(z + delta + 16, 16) < z)
        def _(delta=delta):
            pl.semaphore_signal(z_ready, inc=1, device_id=along_z(delta), device_id_type=MESH)

    gather = Gather(cot, c_full, c_half, c_sf, c_sh, x, y)
    ngather = Gather(norm, n_full, n_half, n_sf, n_sh, x, y)
    sends = []
    stores = []

    def cstart():
        loads[0].wait()
        loads[1].wait()
        gather.start()

    def coords():
        loads[2].wait()
        loads[3].wait()

        def coord_step(i, total):
            cols = pl.ds(pl.multiple_of(i * 1024, 1024), 1024)
            return total + jnp.dot(act[:, cols], basis[cols, :], preferred_element_type=F32)

        total = lax.fori_loop(0, 8, coord_step, jnp.zeros((128, 512), F32))
        ct_own[...] = total.T.astype(BF16)

    def ct_copy(d):
        to = lax.rem(dp + d, 16)
        rows = pl.ds(pl.multiple_of(to * 32, 32), 32)
        return remote(ct_own.at[rows], ct.at[dp], ct_send.at[d], ct_recv.at[dp], {"dp": to})

    def ct_go():
        def ct_start(d, carry):
            ct_copy(d).start()
            return carry

        lax.fori_loop(1, 16, ct_start, 0)
        ct[dp] = ct_own[pl.ds(pl.multiple_of(dp * 32, 32), 32), :]

    def ct_take():
        def ct_wait(d, carry):
            s = lax.rem(dp + d, 16)
            remote(ct.at[s], ct.at[s], ct_send.at[d], ct_recv.at[s], {"dp": s}).wait_recv()
            return carry

        lax.fori_loop(1, 16, ct_wait, 0)
        acc[...] = jnp.zeros_like(acc)

    def places(k):
        return [lax.rem(y + dy, 4) * 4 + lax.rem(x + dx, 4) for dy, dx in ROUNDS[k]]

    def first(k):
        return sum(len(r) for r in ROUNDS[:k])

    def project(k):
        spots = places(k)

        def step(i, carry):
            p = pick(i, spots)
            for g in (0, 1):
                acc[g] += jnp.dot(ct[p], cot[g, p], preferred_element_type=F32)
            return carry

        lax.fori_loop(0, len(spots), step, 0)

    def send(src, dst, ss, rs, dev):
        copy = remote(src, dst, ss, rs, dev)
        copy.start()
        sends.append(copy)

    def take(ref, ss, rs):
        remote(ref, ref, ss, rs, sibling).wait_recv()

    def span(k):
        return pl.ds(first(k) * 64, len(ROUNDS[k]) * 64)

    def bspan(k):
        return pl.ds(first(k) * 16, len(ROUNDS[k]) * 16)

    def chunk(k, steps):
        n = len(ROUNDS[k])
        q = lax.rem(q0 + steps + 4, 4)
        return pl.ds(pl.multiple_of(first(k) * 64 + q * (16 * n), 16), 16 * n)

    def z1(k):
        spots = places(k)

        def step(i, carry):
            p = pick(i, spots)
            part = lax.dot_general(
                cot[0, p], w[0], (((1,), (1,)), ((), ())), preferred_element_type=F32
            )
            part += lax.dot_general(
                cot[1, p], w[1], (((1,), (1,)), ((), ())), preferred_element_type=F32
            )
            tmp[0] = part[:64]
            tmp[1] = part[64:]
            rows = pl.ds(pl.multiple_of((first(k) + i) * 64, 64), 64)
            for r in range(4):
                kept[r, rows] = tmp[c, :, r * 128 : (r + 1) * 128]
                sib_s[r, rows] = tmp[oc, :, r * 128 : (r + 1) * 128].astype(BF16)
            return carry

        if k == 0:
            loads[4].wait()
        lax.fori_loop(0, len(spots), step, 0)
        rows = span(k)
        send(sib_s.at[:, rows], sib_r.at[:, rows], sib_ss.at[k], sib_rs.at[k], sibling)

    def z2(k):
        if ORDER.index(f"z2_{k}") == min(ORDER.index(f"z2_{j}") for j in range(len(ROUNDS))):

            @pl.when(below < len(PARTNERS))
            def _():
                pl.semaphore_wait(z_ready, len(PARTNERS) - below)

        rows = span(k)
        take(sib_r.at[:, rows], sib_ss.at[k], sib_rs.at[k])

        def step(r, carry):
            kept[r, rows] = kept[r, rows] + sib_r[r, rows].astype(F32)
            return carry

        lax.fori_loop(0, 4, step, 0)
        moves = ((2 * up, up), (-up, -up)) if RELAYED[k] else ((up, up), (-up, -up), (2 * up, 2 * up))
        for i, (what, where) in enumerate(moves):
            a_s[i, rows] = kept[kind(what), rows].astype(BF16)
            send(
                a_s.at[i, rows], a_r.at[i, rows], za_s.at[k, i], za_r.at[k, i], along_z(where)
            )

    def z2b(k):
        rows = span(k)
        take(a_r.at[0, rows], za_s.at[k, 0], za_r.at[k, 0])
        a_s[2, rows] = (kept[kind(up), rows] + a_r[0, rows].astype(F32)).astype(BF16)
        send(a_s.at[2, rows], a_r.at[2, rows], za_s.at[k, 2], za_r.at[k, 2], along_z(up))

    def z3(k):
        rows, brows = span(k), bspan(k)
        total = kept[r0, rows]
        for i in (1, 2) if RELAYED[k] else (0, 1, 2):
            take(a_r.at[i, rows], za_s.at[k, i], za_r.at[k, i])
            total = total + a_r[i, rows].astype(F32)
        kept[r0, rows] = total
        moves = (
            ((2, 4 * up), (-up, -4 * up)) if RELAYED[k] else ((up, 4 * up), (-up, -4 * up), (2, 8))
        )
        for i, (what, where) in enumerate(moves):
            b_s[i, brows] = kept[r0, chunk(k, what)].astype(BF16)
            send(
                b_s.at[i, brows], b_r.at[i, brows], zb_s.at[k, i], zb_r.at[k, i], along_z(where)
            )

    def z3b(k):
        brows = bspan(k)
        take(b_r.at[0, brows], zb_s.at[k, 0], zb_r.at[k, 0])
        b_s[2, brows] = (kept[r0, chunk(k, up)] + b_r[0, brows].astype(F32)).astype(BF16)
        send(b_s.at[2, brows], b_r.at[2, brows], zb_s.at[k, 2], zb_r.at[k, 2], along_z(4 * up))

    def z4(k):
        brows = bspan(k)
        total = kept[r0, chunk(k, 0)]
        for i in (1, 2) if RELAYED[k] else (0, 1, 2):
            take(b_r.at[i, brows], zb_s.at[k, i], zb_r.at[k, i])
            total = total + b_r[i, brows].astype(F32)
        out[c, r0, chunk(k, 0)] = total.astype(BF16)
        ref = out.at[c, r0, chunk(k, 0)]
        for i, where in enumerate((4 * up, -4 * up) if RELAYED[k] else (4 * up, -4 * up, 8)):
            send(ref, ref, zc_s.at[k, i], zc_r.at[k, i], along_z(where))

    def z4b(k):
        ref = out.at[c, r0, chunk(k, -up)]
        take(ref, zc_s.at[k, 0], zc_r.at[k, 0])
        send(ref, ref, zc_s.at[k, 2], zc_r.at[k, 2], along_z(4 * up))

    def z5(k):
        for i, steps in enumerate((-up, up, 2)):
            if i > 0 or not RELAYED[k]:
                take(out.at[c, r0, chunk(k, steps)], zc_s.at[k, i], zc_r.at[k, i])
        ref = out.at[c, r0, span(k)]
        for i, where in enumerate((up, -up) if RELAYED[k] else (up, -up, 2 * up)):
            send(ref, ref, zd_s.at[k, i], zd_r.at[k, i], along_z(where))

    def z5b(k):
        ref = out.at[c, kind(-up), span(k)]
        take(ref, zd_s.at[k, 0], zd_r.at[k, 0])
        send(ref, ref, zd_s.at[k, 2], zd_r.at[k, 2], along_z(up))

    def z6(k):
        rows = span(k)
        for i, steps in enumerate((-up, up, 2)):
            if i > 0 or not RELAYED[k]:
                take(out.at[c, kind(steps), rows], zd_s.at[k, i], zd_r.at[k, i])
        ref = out.at[c, :, rows]
        send(ref, ref, ze_s.at[k], ze_r.at[k], sibling)

    def ig_copy(k, i):
        rows = pl.ds(pl.multiple_of(pick(i, places(k)) * 128, 128), 128)
        return pltpu.make_async_copy(ig.at[rows], ig_h.at[rows], store_sem.at[first(k) + i])

    def z7(k):
        take(out.at[oc, :, span(k)], ze_s.at[k], ze_r.at[k])
        spots = places(k)

        def step(i, carry):
            p = pick(i, spots)
            source = pl.ds(pl.multiple_of((first(k) + i) * 64, 64), 64)
            for half in range(2):
                rows = pl.ds(pl.multiple_of(p * 128 + half * 64, 64), 64)
                for r in range(4):
                    ig[rows, r * 128 : (r + 1) * 128] = out[half, r, source]
            ig_copy(k, i).start()
            return carry

        lax.fori_loop(0, len(spots), step, 0)

    def nstart():
        loads[5].wait()
        loads[6].wait()
        loads[7].wait()
        step_value = jnp.full((1, 1), step_s[0].astype(F32), F32)
        first_fix = 1.0 - jnp.exp(step_value * math.log(beta_one))
        second_fix = 1.0 - jnp.exp(step_value * math.log(beta_two))
        for g in (0, 1):
            projected = acc[g]
            first_new = beta_one * m1[g] + (1.0 - beta_one) * projected
            second_new = beta_two * m2[g] + (1.0 - beta_two) * projected * projected
            m1[g] = first_new
            m2[g] = second_new
            norm[g, dp] = (
                first_new / first_fix / (jnp.sqrt(second_new / second_fix) + adam_eps)
            ).astype(BF16)
        ngather.start()
        for ref, dst, i in ((m1, fn_h, 5), (m2, sn_h, 6)):
            store = pltpu.make_async_copy(ref, dst, load_sem.at[i])
            store.start()
            stores.append(store)

    def update():
        rows = pl.ds(pl.multiple_of(dp * 512, 512), 512)
        for g in (0, 1):
            upd[g] = jnp.dot(
                basis[rows, :], norm[g].reshape(512, 896), preferred_element_type=F32
            ).astype(BF16)
            store = pltpu.make_async_copy(upd.at[g], upd_h.at[g], load_sem.at[g])
            store.start()
            stores.append(store)

    steps = dict(
        cstart=cstart, coords=coords, ct=ct_go, ctw=ct_take, nstart=nstart, upd=update,
        pj=project, z1=z1, z2=z2, z2b=z2b, z3=z3, z3b=z3b, z4=z4, z4b=z4b, z5=z5, z5b=z5b,
        z6=z6, z7=z7,
    )
    for name in ORDER:
        if name in steps:
            steps[name]()
        elif "_" in name:
            step, k = name.split("_")
            steps[step](int(k))
        else:
            g, u, v = (int(digit) for digit in name[1:])
            (gather if name[0] == "c" else ngather).step(g, u, v)

    gather.drain()
    ngather.drain()
    for copy in sends:
        copy.wait_send()

    def ct_drain(d, carry):
        ct_copy(d).wait_send()
        return carry

    lax.fori_loop(1, 16, ct_drain, 0)
    for store in stores:
        store.wait()
    for k in range(len(ROUNDS)):

        def stored(i, carry, k=k):
            ig_copy(k, i).wait()
            return carry

        lax.fori_loop(0, len(ROUNDS[k]), stored, 0)


def finish(ig_i, upd_i, m1_i, m2_i, ig_o, upd_o, fn_o, sn_o, sem):
    pairs = [(ig_i.at[pl.ds(j * 512, 512)], ig_o.at[pl.ds(j * 512, 512)]) for j in range(4)]
    pairs += [(upd_i.at[g], upd_o.at[g]) for g in range(2)] + [(m1_i, fn_o), (m2_i, sn_o)]
    copies = [pltpu.make_async_copy(src, dst, sem.at[i]) for i, (src, dst) in enumerate(pairs)]
    for copy in copies:
        copy.start()
    for copy in copies:
        copy.wait()


def local(activations, cotangent, weights, proj_basis, first_moment, second_moment, step_number):
    any_spec = pl.BlockSpec(memory_space=pl.ANY)
    dma = pltpu.SemaphoreType.DMA
    rounds = len(ROUNDS)
    moment = jax.ShapeDtypeStruct((2, 32, 896), F32)
    grad, update, first_new, second_new = pl.pallas_call(
        kernel,
        out_shape=(
            pltpu.VMEM((2048, 512), BF16),
            pltpu.VMEM((2, 512, 896), BF16),
            pltpu.VMEM((2, 32, 896), F32),
            pltpu.VMEM((2, 32, 896), F32),
        ),
        in_specs=[pl.BlockSpec(memory_space=pltpu.HBM)] * 7,
        out_specs=[any_spec] * 4,
        scratch_shapes=[
            pltpu.VMEM((128, 8192), BF16),
            pltpu.VMEM((8192, 512), BF16),
            pltpu.VMEM((2, 512, 896), BF16),
            pltpu.VMEM((2, 32, 896), F32),
            pltpu.VMEM((2, 32, 896), F32),
            pltpu.VMEM((2, 16, 128, 896), BF16),
            pltpu.VMEM((512, 128), BF16),
            pltpu.VMEM((16, 32, 128), BF16),
            pltpu.VMEM((2, 16, 32, 896), BF16),
            pltpu.VMEM((2, 32, 896), F32),
            pltpu.VMEM((2, 64, 512), F32),
            pltpu.VMEM((4, 1024, 128), F32),
            pltpu.VMEM((4, 1024, 128), BF16),
            pltpu.VMEM((4, 1024, 128), BF16),
            pltpu.VMEM((3, 1024, 128), BF16),
            pltpu.VMEM((3, 1024, 128), BF16),
            pltpu.VMEM((3, 256, 128), BF16),
            pltpu.VMEM((3, 256, 128), BF16),
            pltpu.VMEM((2, 4, 1024, 128), BF16),
            pltpu.VMEM((2048, 512), BF16),
            pltpu.VMEM((2, 512, 896), BF16),
            dma((8,)),
            dma((16,)), dma((16,)),
            dma((2, 16)), dma((2, 16, 2)), dma((2, 5, 2)), dma((2, 5, 2)),
            dma((2, 16)), dma((2, 16, 2)), dma((2, 5, 2)), dma((2, 5, 2)),
            dma((rounds,)), dma((rounds,)),
            dma((rounds, 3)), dma((rounds, 3)),
            dma((rounds, 3)), dma((rounds, 3)),
            dma((rounds, 3)), dma((rounds, 3)),
            dma((rounds, 3)), dma((rounds, 3)),
            dma((rounds,)), dma((rounds,)),
            dma((16,)),
            pltpu.SemaphoreType.REGULAR,
            pltpu.SMEM((1,), jnp.int32),
        ],
        compiler_params=pltpu.CompilerParams(
            collective_id=0, has_side_effects=True, vmem_limit_bytes=KERNEL_MIB << 20
        ),
        cost_estimate=pl.CostEstimate(
            flops=6_000_000_000, bytes_accessed=22_000_000, transcendentals=60_000
        ),
    )(activations, cotangent, weights, proj_basis, first_moment, second_moment, step_number)
    return pl.pallas_call(
        finish,
        out_shape=(
            jax.ShapeDtypeStruct((2048, 512), BF16),
            jax.ShapeDtypeStruct((2, 512, 896), BF16),
            moment,
            moment,
        ),
        in_specs=[any_spec] * 4,
        out_specs=[any_spec] * 4,
        scratch_shapes=[dma((8,))],
        compiler_params=pltpu.CompilerParams(vmem_limit_bytes=4 << 20),
        cost_estimate=pl.CostEstimate(flops=0, bytes_accessed=4_500_000, transcendentals=0),
    )(grad, update, first_new, second_new)


def solution(mesh):
    return jax.shard_map(
        local,
        mesh=mesh,
        in_specs=(
            P("dp", None),
            P(None, "dp", "tensor"),
            P(None, "dp", "tensor"),
            P(),
            P(None, "dp", "tensor"),
            P(None, "dp", "tensor"),
            P(),
        ),
        out_specs=(
            P(None, "dp"),
            P(None, "dp", "tensor"),
            P(None, "dp", "tensor"),
            P(None, "dp", "tensor"),
        ),
        check_vma=False,
    )
```

```python
import functools
import math

import jax
import jax.numpy as jnp
from jax import lax
from jax.experimental import pallas as pl
from jax.experimental.pallas import tpu as pltpu
from jax.sharding import PartitionSpec as P

MESH = pl.DeviceIdType.MESH
beta_one = 0.9
beta_two = 0.999
adam_eps = 1e-08

F32 = jnp.float32
KERNEL_MIB = 57
BF16 = jnp.bfloat16

PARTNERS = (1, -1, 2, -2, 4, -4, 8)
ROUNDS = (
    ((0, 0), (0, 1), (0, 3), (1, 0), (3, 0)),
    ((0, 2), (2, 0), (3, 3)),
    ((3, 1), (1, 3), (1, 1)),
    ((3, 2), (1, 2)),
    ((2, 3), (2, 1)),
    ((2, 2),),
)
RELAYED = (True, True, True, False, False, False)
ORDER = (
    "cstart", "coords", "ct", "c030", "c010", "c130", "c110", "c103", "c101", "c003", "c001",
    "z1_0", "c020", "ctw", "pj_0", "c033", "c031", "z2_0", "c133", "c131", "c013", "c011", "z2b_0",
    "c113", "c111", "c120", "z1_2", "z3_0", "c102", "c002", "pj_2", "z2_2", "c132", "z1_1", "z3b_0",
    "c112", "c023", "c021", "pj_1", "z2b_2", "z2_1", "c032", "z1_3", "z4_0", "c123", "c121", "c012",
    "z3_2", "z2b_1", "pj_3", "z2_3", "c022", "z1_4", "pj_4", "c122", "z4b_0", "z3b_2", "z3_1",
    "z2_4", "z1_5", "z3_3", "pj_5", "nstart", "z5_0", "z3b_1", "z4_2", "z2_5", "z3_4", "n030",
    "n010", "n130", "n110", "n103", "n101", "n003", "n001", "z4_3", "z4_1", "n020", "n033", "n031",
    "z3_5", "n133", "n131", "n013", "n011", "z5b_0", "n120", "n113", "n111", "n002", "n102",
    "z4b_2", "z4_4", "n023", "n021", "n132", "n032", "z4b_1", "n012", "z5_3", "z6_0", "n123",
    "n121", "n112", "z4_5", "z5_2", "n022", "z7_0", "z5_1", "n122", "upd", "z5_4", "z6_3", "z5b_2",
    "z5b_1", "z7_3", "z5_5", "z6_4", "z6_2", "z6_1", "z7_4", "z6_5", "z7_2", "z7_1", "z7_5",
)


def remote(src, dst, send, recv, dev):
    return pltpu.make_async_remote_copy(
        src_ref=src, dst_ref=dst, send_sem=send, recv_sem=recv, device_id=dev, device_id_type=MESH
    )


class Gather:
    def __init__(self, buf, full, half, send_full, send_half, x, y):
        self.buf, self.full, self.half = buf, full, half
        self.send_full, self.send_half = send_full, send_half
        self.x, self.y = x, y
        self.rows = buf.shape[2] // 2
        self.sent = []

    def piece(self, g, u, v):
        dy, dx = (v, u) if g == 0 else (u, v)
        return lax.rem(self.y + dy, 4) * 4 + lax.rem(self.x + dx, 4)

    def device(self, g, axis, delta):
        along_x = (axis == 1) == (g == 0)
        if along_x:
            return {"dp": self.y * 4 + lax.rem(self.x + delta, 4)}
        return {"dp": lax.rem(self.y + delta, 4) * 4 + self.x}

    def send(self, g, axis, u, v, delta):
        p = self.piece(g, u, v)
        slot = 0 if axis == 1 else 1 + u
        ref = self.buf.at[g, p]
        copy = remote(
            ref, ref, self.send_full.at[g, slot, delta // 2], self.full.at[g, p],
            self.device(g, axis, delta),
        )
        copy.start()
        self.sent.append(copy)

    def relay(self, g, axis, u, v):
        off = u if axis == 1 else v
        delta, h = (3, 1) if off == 1 else (1, 0)
        p = self.piece(g, u, v)
        slot = 0 if axis == 1 else 1 + u
        ref = self.buf.at[g, p, pl.ds(h * self.rows, self.rows)]
        copy = remote(
            ref, ref, self.send_half.at[g, slot, h], self.half.at[g, p, h],
            self.device(g, axis, delta),
        )
        copy.start()
        self.sent.append(copy)

    def wait_full(self, g, u, v):
        p = self.piece(g, u, v)
        ref = self.buf.at[g, p]
        remote(
            ref, ref, self.send_full.at[g, 0, 0], self.full.at[g, p], self.device(g, 1, 1)
        ).wait_recv()

    def wait_halves(self, g, u, v):
        p = self.piece(g, u, v)
        for h in (0, 1):
            ref = self.buf.at[g, p, pl.ds(h * self.rows, self.rows)]
            remote(
                ref, ref, self.send_half.at[g, 0, 0], self.half.at[g, p, h], self.device(g, 1, 1)
            ).wait_recv()

    def start(self):
        for axis in (1, 2):
            for g in (0, 1):
                for delta in (1, 3):
                    self.send(g, axis, 0, 0, delta)

    def step(self, g, u, v):
        if 2 in (u if v == 0 else v, v):
            self.wait_halves(g, u, v)
        else:
            self.wait_full(g, u, v)
            self.relay(g, 1 if v == 0 else 2, u, v)
        if v == 0:
            for delta in (1, 3):
                self.send(g, 2, u, 0, delta)

    def drain(self):
        for copy in self.sent:
            copy.wait_send()


def pick(index, values):
    out = values[0]
    for i in range(1, len(values)):
        out = jnp.where(index == i, values[i], out)
    return out


def kernel(
    act_h, cot_h, w_h, basis_h, m1_h, m2_h, step_h,
    ig_h, upd_h, fn_h, sn_h,
    act, basis, w, m1, m2, cot, ct_own, ct, norm, acc, tmp, kept, sib_s, sib_r,
    a_s, a_r, b_s, b_r, out, ig, upd,
    load_sem, ct_send, ct_recv, c_full, c_half, c_sf, c_sh, n_full, n_half, n_sf, n_sh,
    sib_ss, sib_rs, za_s, za_r, zb_s, zb_r, zc_s, zc_r, zd_s, zd_r, ze_s, ze_r, store_sem, z_ready, step_s,
):
    dp = lax.axis_index("dp")
    tensor = lax.axis_index("tensor")
    y, x = lax.div(dp, 4), lax.rem(dp, 4)
    z, c = lax.div(tensor, 2), lax.rem(tensor, 2)
    oc = 1 - c
    up = 1 - 2 * c
    r0, q0 = lax.rem(z, 4), lax.div(z, 4)

    def along_z(delta):
        return {"tensor": lax.rem(z + delta + 16, 16) * 2 + c}

    def kind(delta):
        return lax.rem(z + delta + 4, 4)

    sibling = {"tensor": z * 2 + oc}

    loads = [
        pltpu.make_async_copy(cot_h.at[0], cot.at[0, dp], load_sem.at[0]),
        pltpu.make_async_copy(cot_h.at[1], cot.at[1, dp], load_sem.at[1]),
        pltpu.make_async_copy(act_h, act, load_sem.at[2]),
        pltpu.make_async_copy(basis_h, basis, load_sem.at[3]),
        pltpu.make_async_copy(w_h, w, load_sem.at[4]),
        pltpu.make_async_copy(m1_h, m1, load_sem.at[5]),
        pltpu.make_async_copy(m2_h, m2, load_sem.at[6]),
        pltpu.make_async_copy(step_h, step_s, load_sem.at[7]),
    ]
    for load in loads:
        load.start()

    barrier = pltpu.get_barrier_semaphore()

    def greet(d, carry):
        pl.semaphore_signal(
            barrier, inc=1, device_id={"dp": lax.rem(dp + d, 16)}, device_id_type=MESH
        )
        return carry

    lax.fori_loop(1, 16, greet, 0)
    pl.semaphore_signal(barrier, inc=1, device_id=sibling, device_id_type=MESH)
    below = 0
    for delta in PARTNERS:
        above = lax.rem(z + delta + 16, 16) > z
        below = below + jnp.where(above, 0, 1)

        @pl.when(above)
        def _(delta=delta):
            pl.semaphore_signal(barrier, inc=1, device_id=along_z(delta), device_id_type=MESH)

    pl.semaphore_wait(barrier, 16 + below)
    for delta in PARTNERS:

        @pl.when(lax.rem(z + delta + 16, 16) < z)
        def _(delta=delta):
            pl.semaphore_signal(z_ready, inc=1, device_id=along_z(delta), device_id_type=MESH)

    gather = Gather(cot, c_full, c_half, c_sf, c_sh, x, y)
    ngather = Gather(norm, n_full, n_half, n_sf, n_sh, x, y)
    sends = []
    stores = []

    def cstart():
        loads[0].wait()
        loads[1].wait()
        gather.start()

    def coords():
        loads[2].wait()
        loads[3].wait()

        def coord_step(i, total):
            cols = pl.ds(pl.multiple_of(i * 1024, 1024), 1024)
            return total + jnp.dot(act[:, cols], basis[cols, :], preferred_element_type=F32)

        total = lax.fori_loop(0, 8, coord_step, jnp.zeros((128, 512), F32))
        ct_own[...] = total.T.astype(BF16)

    def ct_copy(d):
        to = lax.rem(dp + d, 16)
        rows = pl.ds(pl.multiple_of(to * 32, 32), 32)
        return remote(ct_own.at[rows], ct.at[dp], ct_send.at[d], ct_recv.at[dp], {"dp": to})

    def ct_go():
        def ct_start(d, carry):
            ct_copy(d).start()
            return carry

        lax.fori_loop(1, 16, ct_start, 0)
        ct[dp] = ct_own[pl.ds(pl.multiple_of(dp * 32, 32), 32), :]

    def ct_take():
        def ct_wait(d, carry):
            s = lax.rem(dp + d, 16)
            remote(ct.at[s], ct.at[s], ct_send.at[d], ct_recv.at[s], {"dp": s}).wait_recv()
            return carry

        lax.fori_loop(1, 16, ct_wait, 0)
        acc[...] = jnp.zeros_like(acc)

    def places(k):
        return [lax.rem(y + dy, 4) * 4 + lax.rem(x + dx, 4) for dy, dx in ROUNDS[k]]

    def first(k):
        return sum(len(r) for r in ROUNDS[:k])

    def project(k):
        spots = places(k)

        def step(i, carry):
            p = pick(i, spots)
            for g in (0, 1):
                acc[g] += jnp.dot(ct[p], cot[g, p], preferred_element_type=F32)
            return carry

        lax.fori_loop(0, len(spots), step, 0)

    def send(src, dst, ss, rs, dev):
        copy = remote(src, dst, ss, rs, dev)
        copy.start()
        sends.append(copy)

    def take(ref, ss, rs):
        remote(ref, ref, ss, rs, sibling).wait_recv()

    def span(k):
        return pl.ds(first(k) * 64, len(ROUNDS[k]) * 64)

    def bspan(k):
        return pl.ds(first(k) * 16, len(ROUNDS[k]) * 16)

    def chunk(k, steps):
        n = len(ROUNDS[k])
        q = lax.rem(q0 + steps + 4, 4)
        return pl.ds(pl.multiple_of(first(k) * 64 + q * (16 * n), 16), 16 * n)

    def z1(k):
        spots = places(k)

        def step(i, carry):
            p = pick(i, spots)
            part = lax.dot_general(
                cot[0, p], w[0], (((1,), (1,)), ((), ())), preferred_element_type=F32
            )
            part += lax.dot_general(
                cot[1, p], w[1], (((1,), (1,)), ((), ())), preferred_element_type=F32
            )
            tmp[0] = part[:64]
            tmp[1] = part[64:]
            rows = pl.ds(pl.multiple_of((first(k) + i) * 64, 64), 64)
            for r in range(4):
                kept[r, rows] = tmp[c, :, r * 128 : (r + 1) * 128]
                sib_s[r, rows] = tmp[oc, :, r * 128 : (r + 1) * 128].astype(BF16)
            return carry

        if k == 0:
            loads[4].wait()
        lax.fori_loop(0, len(spots), step, 0)
        rows = span(k)
        send(sib_s.at[:, rows], sib_r.at[:, rows], sib_ss.at[k], sib_rs.at[k], sibling)

    def z2(k):
        if ORDER.index(f"z2_{k}") == min(ORDER.index(f"z2_{j}") for j in range(len(ROUNDS))):

            @pl.when(below < len(PARTNERS))
            def _():
                pl.semaphore_wait(z_ready, len(PARTNERS) - below)

        rows = span(k)
        take(sib_r.at[:, rows], sib_ss.at[k], sib_rs.at[k])

        def total(r):
            return kept[r, rows] + sib_r[r, rows].astype(F32)

        moves = ((2 * up, up), (-up, -up)) if RELAYED[k] else ((up, up), (-up, -up), (2 * up, 2 * up))
        for i, (what, where) in enumerate(moves):
            a_s[i, rows] = total(kind(what)).astype(BF16)
            send(
                a_s.at[i, rows], a_r.at[i, rows], za_s.at[k, i], za_r.at[k, i], along_z(where)
            )
        for r in (r0, kind(up)) if RELAYED[k] else (r0,):
            kept[r, rows] = total(r)

    def z2b(k):
        rows = span(k)
        take(a_r.at[0, rows], za_s.at[k, 0], za_r.at[k, 0])
        a_s[2, rows] = (kept[kind(up), rows] + a_r[0, rows].astype(F32)).astype(BF16)
        send(a_s.at[2, rows], a_r.at[2, rows], za_s.at[k, 2], za_r.at[k, 2], along_z(up))

    def z3(k):
        rows, brows = span(k), bspan(k)
        parts = (1, 2) if RELAYED[k] else (0, 1, 2)
        for i in parts:
            take(a_r.at[i, rows], za_s.at[k, i], za_r.at[k, i])

        def total(steps):
            own = chunk(k, steps)
            return sum((a_r[i, own].astype(F32) for i in parts), kept[r0, own])

        moves = (
            ((2, 4 * up), (-up, -4 * up)) if RELAYED[k] else ((up, 4 * up), (-up, -4 * up), (2, 8))
        )
        for i, (what, where) in enumerate(moves):
            b_s[i, brows] = total(what).astype(BF16)
            send(
                b_s.at[i, brows], b_r.at[i, brows], zb_s.at[k, i], zb_r.at[k, i], along_z(where)
            )
        for steps in (0, up) if RELAYED[k] else (0,):
            kept[r0, chunk(k, steps)] = total(steps)

    def z3b(k):
        brows = bspan(k)
        take(b_r.at[0, brows], zb_s.at[k, 0], zb_r.at[k, 0])
        b_s[2, brows] = (kept[r0, chunk(k, up)] + b_r[0, brows].astype(F32)).astype(BF16)
        send(b_s.at[2, brows], b_r.at[2, brows], zb_s.at[k, 2], zb_r.at[k, 2], along_z(4 * up))

    def z4(k):
        brows = bspan(k)
        total = kept[r0, chunk(k, 0)]
        for i in (1, 2) if RELAYED[k] else (0, 1, 2):
            take(b_r.at[i, brows], zb_s.at[k, i], zb_r.at[k, i])
            total = total + b_r[i, brows].astype(F32)
        out[c, r0, chunk(k, 0)] = total.astype(BF16)
        ref = out.at[c, r0, chunk(k, 0)]
        for i, where in enumerate((4 * up, -4 * up) if RELAYED[k] else (4 * up, -4 * up, 8)):
            send(ref, ref, zc_s.at[k, i], zc_r.at[k, i], along_z(where))

    def z4b(k):
        ref = out.at[c, r0, chunk(k, -up)]
        take(ref, zc_s.at[k, 0], zc_r.at[k, 0])
        send(ref, ref, zc_s.at[k, 2], zc_r.at[k, 2], along_z(4 * up))

    def z5(k):
        for i, steps in enumerate((-up, up, 2)):
            if i > 0 or not RELAYED[k]:
                take(out.at[c, r0, chunk(k, steps)], zc_s.at[k, i], zc_r.at[k, i])
        ref = out.at[c, r0, span(k)]
        for i, where in enumerate((up, -up) if RELAYED[k] else (up, -up, 2 * up)):
            send(ref, ref, zd_s.at[k, i], zd_r.at[k, i], along_z(where))

    def z5b(k):
        ref = out.at[c, kind(-up), span(k)]
        take(ref, zd_s.at[k, 0], zd_r.at[k, 0])
        send(ref, ref, zd_s.at[k, 2], zd_r.at[k, 2], along_z(up))

    def z6(k):
        rows = span(k)
        for i, steps in enumerate((-up, up, 2)):
            if i > 0 or not RELAYED[k]:
                take(out.at[c, kind(steps), rows], zd_s.at[k, i], zd_r.at[k, i])
        ref = out.at[c, :, rows]
        send(ref, ref, ze_s.at[k], ze_r.at[k], sibling)

    def ig_copy(k, i):
        rows = pl.ds(pl.multiple_of(pick(i, places(k)) * 128, 128), 128)
        return pltpu.make_async_copy(ig.at[rows], ig_h.at[rows], store_sem.at[first(k) + i])

    def z7(k):
        take(out.at[oc, :, span(k)], ze_s.at[k], ze_r.at[k])
        spots = places(k)

        def step(i, carry):
            p = pick(i, spots)
            source = pl.ds(pl.multiple_of((first(k) + i) * 64, 64), 64)
            for half in range(2):
                rows = pl.ds(pl.multiple_of(p * 128 + half * 64, 64), 64)
                for r in range(4):
                    ig[rows, r * 128 : (r + 1) * 128] = out[half, r, source]
            ig_copy(k, i).start()
            return carry

        lax.fori_loop(0, len(spots), step, 0)

    def nstart():
        loads[5].wait()
        loads[6].wait()
        loads[7].wait()
        step_value = jnp.full((1, 1), step_s[0].astype(F32), F32)
        first_fix = 1.0 - jnp.exp(step_value * math.log(beta_one))
        second_fix = 1.0 - jnp.exp(step_value * math.log(beta_two))
        for g in (0, 1):
            projected = acc[g]
            first_new = beta_one * m1[g] + (1.0 - beta_one) * projected
            second_new = beta_two * m2[g] + (1.0 - beta_two) * projected * projected
            m1[g] = first_new
            m2[g] = second_new
            norm[g, dp] = (
                first_new / first_fix / (jnp.sqrt(second_new / second_fix) + adam_eps)
            ).astype(BF16)
        ngather.start()
        for ref, dst, i in ((m1, fn_h, 5), (m2, sn_h, 6)):
            store = pltpu.make_async_copy(ref, dst, load_sem.at[i])
            store.start()
            stores.append(store)

    def update():
        rows = pl.ds(pl.multiple_of(dp * 512, 512), 512)
        for g in (0, 1):
            upd[g] = jnp.dot(
                basis[rows, :], norm[g].reshape(512, 896), preferred_element_type=F32
            ).astype(BF16)
            store = pltpu.make_async_copy(upd.at[g], upd_h.at[g], load_sem.at[g])
            store.start()
            stores.append(store)

    steps = dict(
        cstart=cstart, coords=coords, ct=ct_go, ctw=ct_take, nstart=nstart, upd=update,
        pj=project, z1=z1, z2=z2, z2b=z2b, z3=z3, z3b=z3b, z4=z4, z4b=z4b, z5=z5, z5b=z5b,
        z6=z6, z7=z7,
    )
    for name in ORDER:
        if name in steps:
            steps[name]()
        elif "_" in name:
            step, k = name.split("_")
            steps[step](int(k))
        else:
            g, u, v = (int(digit) for digit in name[1:])
            (gather if name[0] == "c" else ngather).step(g, u, v)

    gather.drain()
    ngather.drain()
    for copy in sends:
        copy.wait_send()

    def ct_drain(d, carry):
        ct_copy(d).wait_send()
        return carry

    lax.fori_loop(1, 16, ct_drain, 0)
    for store in stores:
        store.wait()
    for k in range(len(ROUNDS)):

        def stored(i, carry, k=k):
            ig_copy(k, i).wait()
            return carry

        lax.fori_loop(0, len(ROUNDS[k]), stored, 0)


def finish(ig_i, upd_i, m1_i, m2_i, ig_o, upd_o, fn_o, sn_o, sem):
    pairs = [(ig_i.at[pl.ds(j * 512, 512)], ig_o.at[pl.ds(j * 512, 512)]) for j in range(4)]
    pairs += [(upd_i.at[g], upd_o.at[g]) for g in range(2)] + [(m1_i, fn_o), (m2_i, sn_o)]
    copies = [pltpu.make_async_copy(src, dst, sem.at[i]) for i, (src, dst) in enumerate(pairs)]
    for copy in copies:
        copy.start()
    for copy in copies:
        copy.wait()


def local(activations, cotangent, weights, proj_basis, first_moment, second_moment, step_number):
    any_spec = pl.BlockSpec(memory_space=pl.ANY)
    dma = pltpu.SemaphoreType.DMA
    rounds = len(ROUNDS)
    moment = jax.ShapeDtypeStruct((2, 32, 896), F32)
    grad, update, first_new, second_new = pl.pallas_call(
        kernel,
        out_shape=(
            pltpu.VMEM((2048, 512), BF16),
            pltpu.VMEM((2, 512, 896), BF16),
            pltpu.VMEM((2, 32, 896), F32),
            pltpu.VMEM((2, 32, 896), F32),
        ),
        in_specs=[pl.BlockSpec(memory_space=pltpu.HBM)] * 7,
        out_specs=[any_spec] * 4,
        scratch_shapes=[
            pltpu.VMEM((128, 8192), BF16),
            pltpu.VMEM((8192, 512), BF16),
            pltpu.VMEM((2, 512, 896), BF16),
            pltpu.VMEM((2, 32, 896), F32),
            pltpu.VMEM((2, 32, 896), F32),
            pltpu.VMEM((2, 16, 128, 896), BF16),
            pltpu.VMEM((512, 128), BF16),
            pltpu.VMEM((16, 32, 128), BF16),
            pltpu.VMEM((2, 16, 32, 896), BF16),
            pltpu.VMEM((2, 32, 896), F32),
            pltpu.VMEM((2, 64, 512), F32),
            pltpu.VMEM((4, 1024, 128), F32),
            pltpu.VMEM((4, 1024, 128), BF16),
            pltpu.VMEM((4, 1024, 128), BF16),
            pltpu.VMEM((3, 1024, 128), BF16),
            pltpu.VMEM((3, 1024, 128), BF16),
            pltpu.VMEM((3, 256, 128), BF16),
            pltpu.VMEM((3, 256, 128), BF16),
            pltpu.VMEM((2, 4, 1024, 128), BF16),
            pltpu.VMEM((2048, 512), BF16),
            pltpu.VMEM((2, 512, 896), BF16),
            dma((8,)),
            dma((16,)), dma((16,)),
            dma((2, 16)), dma((2, 16, 2)), dma((2, 5, 2)), dma((2, 5, 2)),
            dma((2, 16)), dma((2, 16, 2)), dma((2, 5, 2)), dma((2, 5, 2)),
            dma((rounds,)), dma((rounds,)),
            dma((rounds, 3)), dma((rounds, 3)),
            dma((rounds, 3)), dma((rounds, 3)),
            dma((rounds, 3)), dma((rounds, 3)),
            dma((rounds, 3)), dma((rounds, 3)),
            dma((rounds,)), dma((rounds,)),
            dma((16,)),
            pltpu.SemaphoreType.REGULAR,
            pltpu.SMEM((1,), jnp.int32),
        ],
        compiler_params=pltpu.CompilerParams(
            collective_id=0, has_side_effects=True, vmem_limit_bytes=KERNEL_MIB << 20
        ),
        cost_estimate=pl.CostEstimate(
            flops=6_000_000_000, bytes_accessed=22_000_000, transcendentals=60_000
        ),
    )(activations, cotangent, weights, proj_basis, first_moment, second_moment, step_number)
    return pl.pallas_call(
        finish,
        out_shape=(
            jax.ShapeDtypeStruct((2048, 512), BF16),
            jax.ShapeDtypeStruct((2, 512, 896), BF16),
            moment,
            moment,
        ),
        in_specs=[any_spec] * 4,
        out_specs=[any_spec] * 4,
        scratch_shapes=[dma((8,))],
        compiler_params=pltpu.CompilerParams(vmem_limit_bytes=4 << 20),
        cost_estimate=pl.CostEstimate(flops=0, bytes_accessed=4_500_000, transcendentals=0),
    )(grad, update, first_new, second_new)


def solution(mesh):
    return jax.shard_map(
        local,
        mesh=mesh,
        in_specs=(
            P("dp", None),
            P(None, "dp", "tensor"),
            P(None, "dp", "tensor"),
            P(),
            P(None, "dp", "tensor"),
            P(None, "dp", "tensor"),
            P(),
        ),
        out_specs=(
            P(None, "dp"),
            P(None, "dp", "tensor"),
            P(None, "dp", "tensor"),
            P(None, "dp", "tensor"),
        ),
        check_vma=False,
    )
```
